128 devices in a mesh: row: 16 (over z, x_hi, core), col: 8 (over y, x_lo).
Axes of the slice: x: 4 (x_hi: 2, x_lo: 2; x = x_hi * 2 + x_lo), y: 4, z: 4, core: 2. Of those that a mesh axis runs over, the one named last changes fastest.
Arguments:
- matrix: bfloat16 [8192, 8192], P('row', 'col'), may hold values from -6 to 6
- factors: float32 [8192, 8192], P('row', 'col')
- inverse: bfloat16 [64, 128, 128], P('col'), may hold values from -0.007171631 to 0.007171631
- pattern: int32 [64, 64], P('row', 'col'), may hold values from 0 to 1, as said below
- dropped: int32 [64, 64], P('row', 'col'), may hold values from 0 to 1, as said below
Outputs:
- factors_out: float32 [8192, 8192], P('row', 'col')
The draws below stay inside these ranges and needn't reach their ends.
Inputs may be any that keep to these rules, and one draw needn't show every extreme that they name: Block (I, J) can be in the pattern only where I - J is 0, 1, -1, 4, -4, 32 or -32; the blocks with I - J of 0, 1, -1, 4 and -4 are always in it. In each device's region of 4 block rows by 8 block columns, every block column holds at most 3 pattern blocks (exactly 3 in some columns), and every block row at most 2 pattern blocks below the block diagonal (exactly 2 in some rows). `dropped`: dropped blocks lie in the pattern and off the block diagonal.
All inputs are finite; a program needn't handle non-finite values.
Results may differ from the reference program's by a relative error of at most 0.00083.
Values may be sent and summed in bfloat16 or wider, within the bound.
No kernel may reach another device: no remote copies, remote signals or barrier semaphores. Data moves between devices by JAX's collectives and lax.ppermute only.
A program may use at most 128 MiB of HBM per device.

```python
import jax
import jax.numpy as jnp
from jax import lax

BS = 128
RB = 4
SWEEPS = 2
NB = 64
N = 8192


def pattern_from(key):
    row_number = jnp.arange(NB)[:, None]
    col_number = jnp.arange(NB)[None, :]
    offset = jnp.abs(row_number - col_number)
    band = (offset <= 1) | (offset == RB)
    far = offset == NB // 2
    lowest = jnp.minimum(row_number, col_number)
    coin_vector = jax.random.randint(jax.random.fold_in(key, 11), (NB,), 0, 2)
    keep_far = (coin_vector[lowest] == 1) | (lowest % RB == 0)
    return (band | far & keep_far).astype(jnp.int32)


def draw_pattern(key, part):
    return pattern_from(key)


def draw_dropped(key, part):
    member = pattern_from(key)
    coin = jax.random.randint(jax.random.fold_in(key, 13), (NB, NB), 0, 4) == 0
    row_number = jnp.arange(NB)[:, None]
    col_number = jnp.arange(NB)[None, :]
    off_diagonal = row_number != col_number
    return (member * coin * off_diagonal).astype(jnp.int32)


def draw_factors(key, part):
    block_number = jnp.arange(N) // BS
    below = block_number[:, None] > block_number[None, :]
    spread = jnp.where(below, 0.015, 1.0).astype(jnp.float32)
    raw_values = jax.random.normal(key, (N, N), jnp.float32)
    return (raw_values * spread).astype(jnp.float32)


def block_levels(rng, extent, split, smallest, high):
    factor_of, own = 1.0, jax.random.fold_in(rng, 6)
    for axis_at, blocks in split:
        steps = jnp.exp(jax.random.uniform(jax.random.fold_in(own, axis_at), (blocks,), jnp.float32, smallest / len(split), high / len(split)))
        factor_of = factor_of * jnp.repeat(steps, extent[axis_at] // blocks).reshape([-1 if axis == axis_at else 1 for axis in range(len(extent))])
    return factor_of


def normal_values(own_key, extent, width, bound, split=(), kind=jnp.bfloat16):
    level = block_levels(own_key, extent, split, -0.22, 0.18) if split else 1.0
    entries = jax.random.normal(own_key, extent, jnp.float32) * width * level
    return jnp.minimum(jnp.maximum(entries, -bound), bound).astype(kind)


def setup_inputs(seed: int = 0) -> dict:
    streams_of = jax.random.split(jax.random.key(seed), 6)
    matrix = normal_values(streams_of[0], (N, N), 1.0, 6.0, ((0, 16), (1, 8)))
    factors = draw_factors(jax.random.fold_in(streams_of[5], 71), 0)
    inverse = normal_values(streams_of[2], (NB, BS, BS), 0.0012, 0.007171631, ((0, 8),))
    pattern = draw_pattern(jax.random.fold_in(streams_of[5], 71), 0)
    dropped = draw_dropped(jax.random.fold_in(streams_of[5], 71), 0)
    return {"matrix": matrix, "factors": factors, "inverse": inverse, "pattern": pattern, "dropped": dropped}


def expand(block_mask):
    return jnp.repeat(jnp.repeat(block_mask, BS, axis=0), BS, axis=1)


def reference(matrix, factors, inverse, pattern, dropped):
    row_number = jnp.arange(NB)[:, None]
    col_number = jnp.arange(NB)[None, :]
    member = pattern == 1
    lower_mask = expand((member & (row_number > col_number)).astype(jnp.float32))
    upper_mask = expand((member & (row_number <= col_number)).astype(jnp.float32))
    in_pattern = expand(member.astype(jnp.float32))
    low_part = factors * lower_mask
    up_part = factors * upper_mask
    dense_matrix = matrix.astype(jnp.float32)
    inverse_full = inverse.astype(jnp.float32)
    for sweep_index in range(SWEEPS):
        low_half = lax.optimization_barrier(low_part.astype(jnp.bfloat16)).astype(jnp.float32)
        up_half = lax.optimization_barrier(up_part.astype(jnp.bfloat16)).astype(jnp.float32)
        product = jnp.dot(low_half, up_half, precision=lax.Precision.HIGHEST)
        residual = (dense_matrix - product - up_part) * in_pattern
        rounded = lax.optimization_barrier(residual.astype(jnp.bfloat16)).astype(jnp.float32)
        rounded = rounded.reshape(N, NB, BS)
        correction = jnp.einsum("rjb,jbc->rjc", rounded, inverse_full, precision=lax.Precision.HIGHEST)
        low_part = low_part + correction.reshape(N, N) * lower_mask
        up_part = up_part + residual * upper_mask
    keep_mask = expand((1 - dropped).astype(jnp.float32))
    return (low_part + up_part) * keep_mask
```

```python
import functools

import jax
import jax.numpy as jnp
from jax import lax
from jax.experimental import pallas as pl
from jax.experimental.pallas import tpu as pltpu
from jax.sharding import PartitionSpec as P

BS = 128
F32 = jnp.float32
BF16 = jnp.bfloat16

DIAG, RIGHT, LEFT, X, OFF = 0, 4, 7, 10, 11
SLOTS = 15


def role():
    r, c = lax.axis_index("row"), lax.axis_index("col")
    odd = lax.rem(r, 2)
    home = lax.div(r, 2)
    is_d = c == home
    is_n = jnp.where(odd == 1, c == home + 1, c == home - 1)
    is_f = jnp.where(r < 8, c == home + 4, c == home - 4)
    even = odd == 0
    return dict(
        odd=odd,
        even=even,
        d=is_d,
        n=is_n,
        f=is_f,
        near=is_d | is_n,
        any=is_d | is_n | is_f,
        late=r >= 8,
        lower=(is_d & (odd == 1)) | (is_n & even) | (is_f & (r >= 8)),
        first=4 * odd,
        off=jnp.where(is_f, 4 * odd, 4 * (1 - odd)),
        x_row=jnp.where(odd == 1, jnp.where(is_d, 0, 3), jnp.where(is_d, 3, 0)),
        x_col=jnp.where(odd == 1, jnp.where(is_d, 3, 0), jnp.where(is_d, 4, 7)),
    )


def places(w):
    out = []
    for j in range(4):
        out.append((DIAG + j, j, w["first"] + j, "d"))
    for j in range(3):
        out.append((RIGHT + j, j, w["first"] + j + 1, "d"))
    for j in range(3):
        out.append((LEFT + j, j + 1, w["first"] + j, "d"))
    out.append((X, w["x_row"], w["x_col"], "near"))
    for j in range(4):
        out.append((OFF + j, j, w["off"] + j, "any"))
    return out


def block(ref, i, c):
    return ref.at[pl.ds(pl.multiple_of(i * BS, BS), BS), pl.ds(pl.multiple_of(c * BS, BS), BS)]


def grouped(w, todo):
    for name in ("d", "near", "any"):
        some = [t for t in todo if t[0] == name]
        if some:

            @pl.when(w[name])
            def _():
                for _, act in some:
                    act()


def fetch_blocks(w, src, dst, sem, start):
    def act(slot, i, c):
        copy = pltpu.make_async_copy(block(src, i, c), dst.at[slot], sem)
        copy.start() if start else copy.wait()

    grouped(w, [(g, functools.partial(act, s, i, c)) for s, i, c, g in places(w)])


def masked(w, f, table):
    def act(slot, i, c):
        f[slot] = f[slot] * (table[i, c] == 1).astype(F32)

    grouped(w, [(g, functools.partial(act, s, i, c)) for s, i, c, g in places(w)])


def send_blocks(w, f, sa, sb, sc, sd):
    def put(dst, at, slot):
        dst[at] = f[slot].astype(BF16)

    def off_x(dst):
        for j in range(4):
            put(dst, j, OFF + j)
        put(dst, 4, X)

    def off(dst):
        for j in range(4):
            put(dst, j, OFF + j)

    def diag(dst):
        for j in range(4):
            put(dst, j, DIAG + j)

    @pl.when(w["d"])
    def _():
        diag(sc)

        @pl.when(w["even"])
        def _():
            off_x(sa)
            diag(sb)

        @pl.when(jnp.logical_not(w["even"]))
        def _():
            diag(sa)

    @pl.when(w["n"])
    def _():
        @pl.when(w["even"])
        def _():
            off_x(sb)

        @pl.when(jnp.logical_not(w["even"]))
        def _():
            off_x(sa)

    @pl.when(w["f"])
    def _():
        @pl.when(w["late"])
        def _():
            off(sd)

        @pl.when(jnp.logical_not(w["late"]))
        def _():
            off(sc)


def receive(w, ra, rb, rc, rd, lb, ub, ud, sem, start):
    def go(src, dst):
        copy = pltpu.make_async_copy(src, dst, sem)
        copy.start() if start else copy.wait()

    def middle(ref, j, k):
        return ref.at[j, pl.ds(k * BS, BS), :]

    def side(ref, j, k):
        return ref.at[j, :, pl.ds(k * BS, BS)]

    @pl.when(w["d"])
    def _():
        go(ra.at[4], middle(ub, 0, 0))
        for j in range(4):
            go(ra.at[j], middle(ub, j, 1))

        @pl.when(w["even"])
        def _():
            go(rb.at[4], side(lb, 0, 0))
            for j in range(4):
                go(rb.at[j], side(lb, j, 1))

        @pl.when(jnp.logical_not(w["even"]))
        def _():
            go(rb.at[pl.ds(0, 4)], ud)

        @pl.when(w["late"])
        def _():
            for j in range(4):
                go(rc.at[j], middle(ub, j, 2))
                go(rd.at[j], side(lb, j, 2))

    @pl.when(w["n"] & w["even"])
    def _():
        go(ra.at[pl.ds(0, 4)], ud)

    @pl.when(w["f"] & w["late"])
    def _():
        go(rc, ud)


def sweep(w, f, a, inv, table, lb, ub, ud):
    def member(i, c):
        return (table[i, c] == 1).astype(F32)

    def lower_update(slot, i, c, u, inv_block):
        old = f[slot]
        product = jnp.dot(old.astype(BF16), u, preferred_element_type=F32)
        residual = (a[slot].astype(F32) - product) * member(i, c)
        step = jnp.dot(residual.astype(BF16), inv_block, preferred_element_type=F32)
        f[slot] = old + step * member(i, c)

    def upper_update(slot, i, c):
        old = f[slot]
        f[slot] = old + (a[slot].astype(F32) - old) * member(i, c)

    spots = {s: (i, c) for s, i, c, _ in places(w)}

    @pl.when(w["d"])
    def _():
        for j in range(3):
            lb[j + 1, :, pl.ds(0, BS)] = f[LEFT + j].astype(BF16)
            ub[j + 1, pl.ds(0, BS), :] = f[RIGHT + j].astype(BF16)

        @pl.when(jnp.logical_not(w["even"]))
        def _():
            lb[0, :, pl.ds(0, BS)] = f[X].astype(BF16)
            for j in range(4):
                lb[j, :, pl.ds(BS, BS)] = f[OFF + j].astype(BF16)

        @pl.when(jnp.logical_not(w["late"]))
        def _():
            for j in range(4):
                lb[j, :, pl.ds(2 * BS, BS)] = jnp.zeros((BS, BS), BF16)
                ub[j, pl.ds(2 * BS, BS), :] = jnp.zeros((BS, BS), BF16)

        for j in range(3):
            lower_update(LEFT + j, *spots[LEFT + j], f[DIAG + j].astype(BF16), inv[w["first"] + j])
        for j in range(3):
            upper_update(RIGHT + j, *spots[RIGHT + j])
        for j in range(4):
            i, c = spots[DIAG + j]
            old = f[DIAG + j]
            product = jnp.dot(lb[j], ub[j], preferred_element_type=F32)
            residual = (a[DIAG + j].astype(F32) - product - old) * member(i, c)
            f[DIAG + j] = old + residual

    @pl.when(w["lower"])
    def _():
        for j in range(4):
            lower_update(OFF + j, *spots[OFF + j], ud[j], inv[w["off"] + j])

        @pl.when(w["near"])
        def _():
            lower_update(X, *spots[X], ud[3], inv[w["off"] + 3])

    @pl.when(w["any"] & jnp.logical_not(w["lower"]))
    def _():
        for j in range(4):
            upper_update(OFF + j, *spots[OFF + j])

        @pl.when(w["near"])
        def _():
            upper_update(X, *spots[X])


def first_kernel(pattern, factors, sa, sb, sc, sd, table, f, sem, table_sem):
    w = role()

    @pl.when(w["any"])
    def _():
        get_table = pltpu.make_async_copy(pattern, table, table_sem)
        get_table.start()
        fetch_blocks(w, factors, f, sem, True)
        get_table.wait()
        fetch_blocks(w, factors, f, sem, False)
        masked(w, f, table)
        send_blocks(w, f, sa, sb, sc, sd)


def middle_kernel(pattern, factors, matrix, inverse, ra, rb, rc, rd, sa, sb, sc, sd, state,
                  table, f, a, inv, lb, ub, ud, sems):
    w = role()

    @pl.when(w["any"])
    def _():
        get_table = pltpu.make_async_copy(pattern, table, sems.at[0])
        get_inv = pltpu.make_async_copy(inverse, inv, sems.at[1])
        get_table.start()
        fetch_blocks(w, factors, f, sems.at[2], True)
        receive(w, ra, rb, rc, rd, lb, ub, ud, sems.at[4], True)
        fetch_blocks(w, matrix, a, sems.at[3], True)
        get_inv.start()
        get_table.wait()
        fetch_blocks(w, factors, f, sems.at[2], False)
        masked(w, f, table)
        receive(w, ra, rb, rc, rd, lb, ub, ud, sems.at[4], False)
        fetch_blocks(w, matrix, a, sems.at[3], False)
        get_inv.wait()
        sweep(w, f, a, inv, table, lb, ub, ud)
        keep = pltpu.make_async_copy(f, state, sems.at[2])
        keep.start()
        send_blocks(w, f, sa, sb, sc, sd)
        keep.wait()


def zero_kernel(out, zeros, sem):
    zeros[...] = jnp.zeros_like(zeros)
    rows = zeros.shape[0]
    copies = [
        pltpu.make_async_copy(zeros, out.at[pl.ds(k * rows, rows)], sem)
        for k in range(out.shape[0] // rows)
    ]
    for copy in copies:
        copy.start()
    for copy in copies:
        copy.wait()


def last_kernel(pattern, dropped, matrix, inverse, state, ra, rb, rc, rd, zeroed, out,
                table, drops, f, a, inv, lb, ub, ud, sems):
    del zeroed
    w = role()

    @pl.when(w["any"])
    def _():
        get_table = pltpu.make_async_copy(pattern, table, sems.at[0])
        get_drops = pltpu.make_async_copy(dropped, drops, sems.at[5])
        get_inv = pltpu.make_async_copy(inverse, inv, sems.at[1])
        get_state = pltpu.make_async_copy(state, f, sems.at[2])
        get_table.start()
        get_drops.start()
        get_state.start()
        receive(w, ra, rb, rc, rd, lb, ub, ud, sems.at[4], True)
        fetch_blocks(w, matrix, a, sems.at[3], True)
        get_inv.start()
        get_table.wait()
        get_drops.wait()
        get_state.wait()
        receive(w, ra, rb, rc, rd, lb, ub, ud, sems.at[4], False)
        fetch_blocks(w, matrix, a, sems.at[3], False)
        get_inv.wait()
        sweep(w, f, a, inv, table, lb, ub, ud)

        def write(slot, i, c):
            f[slot] = f[slot] * (1 - drops[i, c]).astype(F32)
            pltpu.make_async_copy(f.at[slot], block(out, i, c), sems.at[2]).start()

        def done(slot, i, c):
            pltpu.make_async_copy(f.at[slot], block(out, i, c), sems.at[2]).wait()

        for act in (write, done):
            grouped(w, [(g, functools.partial(act, s, i, c)) for s, i, c, g in places(w)])


def routes(cols):
    def at(r, c):
        return r * cols + c

    a, b, c8, d = [], [], [], []
    for r in range(16):
        home = r // 2
        if r % 2 == 0:
            a.append((at(r, home), at(r + 1, home)))
            b.append((at(r, home), at(r + 1, home)))
            if r > 0:
                b.append((at(r, home - 1), at(r, home)))
        elif r < 15:
            a.append((at(r, home), at(r + 1, home)))
            a.append((at(r, home + 1), at(r + 1, home + 1)))
        if r < 8:
            c8.append((at(r, home), at(r + 8, home)))
            c8.append((at(r, home + 4), at(r + 8, home + 4)))
        else:
            d.append((at(r, home - 4), at(r, home)))
    return a, b, c8, d


def exchange(buffers):
    return [
        lax.ppermute(x, ("row", "col"), route)
        for x, route in zip(buffers, routes(lax.axis_size("col")))
    ]


ANY = pl.BlockSpec(memory_space=pl.ANY)
VM = pl.BlockSpec(memory_space=pltpu.VMEM)
SENT = [jax.ShapeDtypeStruct((n, BS, BS), BF16) for n in (5, 5, 4, 4)]
MIB = 1 << 20


def params():
    return pltpu.CompilerParams(vmem_limit_bytes=24 * MIB)


def on_device(matrix, factors, inverse, pattern, dropped):
    blocks = pltpu.VMEM((SLOTS, BS, BS), F32)
    halves = pltpu.VMEM((SLOTS, BS, BS), BF16)
    table = pltpu.SMEM(pattern.shape, jnp.int32)
    operands = [
        pltpu.VMEM(inverse.shape, BF16),
        pltpu.VMEM((4, BS, 3 * BS), BF16),
        pltpu.VMEM((4, 3 * BS, BS), BF16),
        pltpu.VMEM((4, BS, BS), BF16),
    ]
    sem = pltpu.SemaphoreType.DMA

    sent = pl.pallas_call(
        first_kernel,
        out_shape=SENT,
        in_specs=[ANY] * 2,
        out_specs=[VM] * 4,
        scratch_shapes=[table, blocks, sem, sem],
        compiler_params=params(),
        name="first",
    )(pattern, factors)
    got = exchange(sent)
    zeroed = pl.pallas_call(
        zero_kernel,
        out_shape=jax.ShapeDtypeStruct(factors.shape, F32),
        out_specs=ANY,
        scratch_shapes=[pltpu.VMEM((64, factors.shape[1]), F32), sem],
        compiler_params=params(),
        cost_estimate=pl.CostEstimate(flops=0, bytes_accessed=factors.size * 4, transcendentals=0),
        name="zeros",
    )()
    *sent, state = pl.pallas_call(
        middle_kernel,
        out_shape=[*SENT, jax.ShapeDtypeStruct((SLOTS, BS, BS), F32)],
        in_specs=[ANY] * 8,
        out_specs=[VM] * 4 + [ANY],
        scratch_shapes=[table, blocks, halves, *operands, pltpu.SemaphoreType.DMA((5,))],
        compiler_params=params(),
        name="middle",
    )(pattern, factors, matrix, inverse, *got)
    got = exchange(sent)
    return pl.pallas_call(
        last_kernel,
        out_shape=jax.ShapeDtypeStruct(factors.shape, F32),
        in_specs=[ANY] * 10,
        out_specs=ANY,
        scratch_shapes=[table, table, blocks, halves, *operands, pltpu.SemaphoreType.DMA((6,))],
        input_output_aliases={9: 0},
        compiler_params=params(),
        name="last",
    )(pattern, dropped, matrix, inverse, state, *got, zeroed)


def solution(mesh):
    placed = (
        P("row", "col"),
        P("row", "col"),
        P("col", None, None),
        P("row", "col"),
        P("row", "col"),
    )
    return jax.shard_map(
        on_device, mesh=mesh, in_specs=placed, out_specs=P("row", "col"), check_vma=False
    )
```

```python
import functools

import jax
import jax.numpy as jnp
import numpy as np
from jax import lax
from jax.experimental import pallas as pl
from jax.experimental.pallas import tpu as pltpu
from jax.sharding import PartitionSpec as P

BS = 128
F32 = jnp.float32
BF16 = jnp.bfloat16

DIAG, RIGHT, LEFT, X, OFF = 0, 4, 7, 10, 11
SLOTS = 15


def role():
    r, c = lax.axis_index("row"), lax.axis_index("col")
    odd = lax.rem(r, 2)
    home = lax.div(r, 2)
    is_d = c == home
    is_n = jnp.where(odd == 1, c == home + 1, c == home - 1)
    is_f = jnp.where(r < 8, c == home + 4, c == home - 4)
    even = odd == 0
    return dict(
        odd=odd,
        even=even,
        d=is_d,
        n=is_n,
        f=is_f,
        near=is_d | is_n,
        any=is_d | is_n | is_f,
        late=r >= 8,
        lower=(is_d & (odd == 1)) | (is_n & even) | (is_f & (r >= 8)),
        first=4 * odd,
        off=jnp.where(is_f, 4 * odd, 4 * (1 - odd)),
        x_row=jnp.where(odd == 1, jnp.where(is_d, 0, 3), jnp.where(is_d, 3, 0)),
        x_col=jnp.where(odd == 1, jnp.where(is_d, 3, 0), jnp.where(is_d, 4, 7)),
    )


def places(w):
    out = []
    for j in range(4):
        out.append((DIAG + j, j, w["first"] + j, "d"))
    for j in range(3):
        out.append((RIGHT + j, j, w["first"] + j + 1, "d"))
    for j in range(3):
        out.append((LEFT + j, j + 1, w["first"] + j, "d"))
    out.append((X, w["x_row"], w["x_col"], "near"))
    for j in range(4):
        out.append((OFF + j, j, w["off"] + j, "any"))
    return out


def block(ref, i, c):
    return ref.at[pl.ds(pl.multiple_of(i * BS, BS), BS), pl.ds(pl.multiple_of(c * BS, BS), BS)]


def grouped(w, todo):
    for name in ("d", "near", "any"):
        some = [t for t in todo if t[0] == name]
        if some:

            @pl.when(w[name])
            def _():
                for _, act in some:
                    act()


def fetch_blocks(w, src, dst, sem, start):
    def act(slot, i, c):
        copy = pltpu.make_async_copy(block(src, i, c), dst.at[slot], sem)
        copy.start() if start else copy.wait()

    grouped(w, [(g, functools.partial(act, s, i, c)) for s, i, c, g in places(w)])


def masked(w, f, table):
    def act(slot, i, c):
        f[slot] = f[slot] * (table[i, c] == 1).astype(F32)

    grouped(w, [(g, functools.partial(act, s, i, c)) for s, i, c, g in places(w)])


def send_blocks(w, f, sa, sb, sc, sd):
    def put(dst, at, slot):
        dst[at] = f[slot].astype(BF16)

    def off_x(dst):
        for j in range(4):
            put(dst, j, OFF + j)
        put(dst, 4, X)

    def off(dst):
        for j in range(4):
            put(dst, j, OFF + j)

    def diag(dst):
        for j in range(4):
            put(dst, j, DIAG + j)

    @pl.when(w["d"])
    def _():
        diag(sc)

        @pl.when(w["even"])
        def _():
            off_x(sa)
            diag(sb)

        @pl.when(jnp.logical_not(w["even"]))
        def _():
            diag(sa)

    @pl.when(w["n"])
    def _():
        @pl.when(w["even"])
        def _():
            off_x(sb)

        @pl.when(jnp.logical_not(w["even"]))
        def _():
            off_x(sa)

    @pl.when(w["f"])
    def _():
        @pl.when(w["late"])
        def _():
            off(sc)

        @pl.when(jnp.logical_not(w["late"]))
        def _():
            off(sd)


def receive(w, ra, rb, rc, rd, lb, ub, ud, sem, start):
    def go(src, dst):
        copy = pltpu.make_async_copy(src, dst, sem)
        copy.start() if start else copy.wait()

    def middle(ref, j, k):
        return ref.at[j, pl.ds(k * BS, BS), :]

    def side(ref, j, k):
        return ref.at[j, :, pl.ds(k * BS, BS)]

    @pl.when(w["d"])
    def _():
        go(ra.at[4], middle(ub, 0, 0))
        for j in range(4):
            go(ra.at[j], middle(ub, j, 1))

        @pl.when(w["even"])
        def _():
            go(rb.at[4], side(lb, 0, 0))
            for j in range(4):
                go(rb.at[j], side(lb, j, 1))

        @pl.when(jnp.logical_not(w["even"]))
        def _():
            go(rb.at[pl.ds(0, 4)], ud)

        @pl.when(w["late"])
        def _():
            for j in range(4):
                go(rd.at[j], middle(ub, j, 2))
                go(rc.at[j], side(lb, j, 2))

    @pl.when(w["n"] & w["even"])
    def _():
        go(ra.at[pl.ds(0, 4)], ud)

    @pl.when(w["f"] & w["late"])
    def _():
        go(rc, ud)


def sweep(w, f, a, inv, table, lb, ub, ud):
    def member(i, c):
        return (table[i, c] == 1).astype(F32)

    def lower_update(slot, i, c, u, inv_block):
        old = f[slot]
        product = jnp.dot(old.astype(BF16), u, preferred_element_type=F32)
        residual = (a[slot].astype(F32) - product) * member(i, c)
        step = jnp.dot(residual.astype(BF16), inv_block, preferred_element_type=F32)
        f[slot] = old + step * member(i, c)

    def upper_update(slot, i, c):
        old = f[slot]
        f[slot] = old + (a[slot].astype(F32) - old) * member(i, c)

    spots = {s: (i, c) for s, i, c, _ in places(w)}

    @pl.when(w["d"])
    def _():
        for j in range(3):
            lb[j + 1, :, pl.ds(0, BS)] = f[LEFT + j].astype(BF16)
            ub[j + 1, pl.ds(0, BS), :] = f[RIGHT + j].astype(BF16)

        @pl.when(jnp.logical_not(w["even"]))
        def _():
            lb[0, :, pl.ds(0, BS)] = f[X].astype(BF16)
            for j in range(4):
                lb[j, :, pl.ds(BS, BS)] = f[OFF + j].astype(BF16)

        @pl.when(jnp.logical_not(w["late"]))
        def _():
            for j in range(4):
                lb[j, :, pl.ds(2 * BS, BS)] = jnp.zeros((BS, BS), BF16)
                ub[j, pl.ds(2 * BS, BS), :] = jnp.zeros((BS, BS), BF16)

        for j in range(3):
            lower_update(LEFT + j, *spots[LEFT + j], f[DIAG + j].astype(BF16), inv[w["first"] + j])
        for j in range(3):
            upper_update(RIGHT + j, *spots[RIGHT + j])
        for j in range(4):
            i, c = spots[DIAG + j]
            old = f[DIAG + j]
            product = jnp.dot(lb[j], ub[j], preferred_element_type=F32)
            residual = (a[DIAG + j].astype(F32) - product - old) * member(i, c)
            f[DIAG + j] = old + residual

    @pl.when(w["lower"])
    def _():
        for j in range(4):
            lower_update(OFF + j, *spots[OFF + j], ud[j], inv[w["off"] + j])

        @pl.when(w["near"])
        def _():
            lower_update(X, *spots[X], ud[3], inv[w["off"] + 3])

    @pl.when(w["any"] & jnp.logical_not(w["lower"]))
    def _():
        for j in range(4):
            upper_update(OFF + j, *spots[OFF + j])

        @pl.when(w["near"])
        def _():
            upper_update(X, *spots[X])


def first_kernel(pattern, factors, sa, sb, sc, sd, table, f, sem, table_sem):
    w = role()

    @pl.when(w["any"])
    def _():
        get_table = pltpu.make_async_copy(pattern, table, table_sem)
        get_table.start()
        fetch_blocks(w, factors, f, sem, True)
        get_table.wait()
        fetch_blocks(w, factors, f, sem, False)
        masked(w, f, table)
        send_blocks(w, f, sa, sb, sc, sd)


def middle_kernel(pattern, factors, matrix, inverse, ra, rb, rc, rd, sa, sb, sc, sd, state,
                  table, f, a, inv, lb, ub, ud, sems):
    w = role()

    @pl.when(w["any"])
    def _():
        get_table = pltpu.make_async_copy(pattern, table, sems.at[0])
        get_inv = pltpu.make_async_copy(inverse, inv, sems.at[1])
        get_table.start()
        fetch_blocks(w, factors, f, sems.at[2], True)
        receive(w, ra, rb, rc, rd, lb, ub, ud, sems.at[4], True)
        fetch_blocks(w, matrix, a, sems.at[3], True)
        get_inv.start()
        get_table.wait()
        fetch_blocks(w, factors, f, sems.at[2], False)
        masked(w, f, table)
        receive(w, ra, rb, rc, rd, lb, ub, ud, sems.at[4], False)
        fetch_blocks(w, matrix, a, sems.at[3], False)
        get_inv.wait()
        sweep(w, f, a, inv, table, lb, ub, ud)
        keep = pltpu.make_async_copy(f, state, sems.at[2])
        keep.start()
        send_blocks(w, f, sa, sb, sc, sd)
        keep.wait()


def zero_kernel(out, zeros, sem):
    zeros[...] = jnp.zeros_like(zeros)
    rows = zeros.shape[0]
    copies = [
        pltpu.make_async_copy(zeros, out.at[pl.ds(k * rows, rows)], sem)
        for k in range(out.shape[0] // rows)
    ]
    for copy in copies:
        copy.start()
    for copy in copies:
        copy.wait()


def last_kernel(pattern, dropped, matrix, inverse, state, ra, rb, rc, rd, zeroed, out,
                table, drops, f, a, inv, lb, ub, ud, sems):
    del zeroed
    w = role()

    @pl.when(w["any"])
    def _():
        get_table = pltpu.make_async_copy(pattern, table, sems.at[0])
        get_drops = pltpu.make_async_copy(dropped, drops, sems.at[5])
        get_inv = pltpu.make_async_copy(inverse, inv, sems.at[1])
        get_state = pltpu.make_async_copy(state, f, sems.at[2])
        get_table.start()
        get_drops.start()
        get_state.start()
        receive(w, ra, rb, rc, rd, lb, ub, ud, sems.at[4], True)
        fetch_blocks(w, matrix, a, sems.at[3], True)
        get_inv.start()
        get_table.wait()
        get_drops.wait()
        get_state.wait()
        receive(w, ra, rb, rc, rd, lb, ub, ud, sems.at[4], False)
        fetch_blocks(w, matrix, a, sems.at[3], False)
        get_inv.wait()
        sweep(w, f, a, inv, table, lb, ub, ud)

        def write(slot, i, c):
            f[slot] = f[slot] * (1 - drops[i, c]).astype(F32)
            pltpu.make_async_copy(f.at[slot], block(out, i, c), sems.at[2]).start()

        def done(slot, i, c):
            pltpu.make_async_copy(f.at[slot], block(out, i, c), sems.at[2]).wait()

        for act in (write, done):
            grouped(w, [(g, functools.partial(act, s, i, c)) for s, i, c, g in places(w)])


def matched(cost):
    n = len(cost)
    u, v = np.zeros(n + 1), np.zeros(n + 1)
    owner = np.zeros(n + 1, int)
    for i in range(1, n + 1):
        owner[0], j0 = i, 0
        best = np.full(n + 1, np.inf)
        back = np.zeros(n + 1, int)
        used = np.zeros(n + 1, bool)
        while owner[j0]:
            used[j0] = True
            i0 = owner[j0]
            slack = cost[i0 - 1] - u[i0] - v[1:]
            better = ~used[1:] & (slack < best[1:])
            best[1:][better] = slack[better]
            back[1:][better] = j0
            j1 = int(np.argmin(np.where(used, np.inf, best)))
            delta = best[j1]
            u[owner[used]] += delta
            v[used] -= delta
            best[~used] -= delta
            j0 = j1
        while j0:
            owner[j0] = owner[back[j0]]
            j0 = back[j0]
    return {int(owner[j]) - 1: j - 1 for j in range(1, n + 1)}


def distance(a, b):
    def chip(i):
        r, c = divmod(i, 8)
        return ((r // 2) % 2) * 2 + c % 2, c // 2, r // 4

    return sum(min(abs(p - q), 4 - abs(p - q)) for p, q in zip(chip(a), chip(b)))


def whole(pairs, busy):
    sends, takes = {a for a, _ in pairs}, {b for _, b in pairs}
    free_a = [i for i in range(128) if i not in sends]
    free_b = [i for i in range(128) if i not in takes]

    def price(a, b):
        if a == b:
            return 1e6
        far = distance(a, b)
        return (2 + far if far else 1) ** 2 * sum(10 if i in busy else 1 for i in (a, b))

    pick = matched(np.array([[price(a, b) for b in free_b] for a in free_a], float))
    return list(pairs) + [(a, free_b[pick[i]]) for i, a in enumerate(free_a)]


def routes():
    def at(r, c):
        return r * 8 + c

    diag = [at(r, r // 2) for r in range(16)]
    near = {r: at(r, r // 2 + (1 if r % 2 else -1)) for r in range(1, 15)}
    far = [at(r, r // 2 + (4 if r < 8 else -4)) for r in range(16)]
    busy = {*diag, *near.values(), *far}
    pair = [(diag[r], diag[r + 1]) for r in range(0, 16, 2)]
    a = pair + [(diag[r], near[r + 1]) for r in range(1, 14, 2)]
    a += [(near[r], diag[r + 1]) for r in range(1, 14, 2)]
    b = pair + [(near[r], diag[r]) for r in range(2, 15, 2)]
    c, d = [], []
    for r in range(8):
        ring = [diag[r], far[r + 8], diag[r + 8], far[r]]
        c += list(zip(ring, ring[1:] + ring[:1]))
        d += [(far[r], diag[r + 8]), (diag[r + 8], far[r])]
    return [whole(x, busy) for x in (a, b, c, d)]


def exchange(buffers):
    out = [None] * 4
    for k in ORDER:
        out[k] = lax.ppermute(buffers[k], ("row", "col"), ROUTES[k])
    return out


ROUTES = routes()
ORDER = (1, 0, 2, 3)
ANY = pl.BlockSpec(memory_space=pl.ANY)
VM = pl.BlockSpec(memory_space=pltpu.VMEM)
SENT = [jax.ShapeDtypeStruct((n, BS, BS), BF16) for n in (5, 5, 4, 4)]
MIB = 1 << 20


def params():
    return pltpu.CompilerParams(vmem_limit_bytes=24 * MIB)


def on_device(matrix, factors, inverse, pattern, dropped):
    blocks = pltpu.VMEM((SLOTS, BS, BS), F32)
    halves = pltpu.VMEM((SLOTS, BS, BS), BF16)
    table = pltpu.SMEM(pattern.shape, jnp.int32)
    operands = [
        pltpu.VMEM(inverse.shape, BF16),
        pltpu.VMEM((4, BS, 3 * BS), BF16),
        pltpu.VMEM((4, 3 * BS, BS), BF16),
        pltpu.VMEM((4, BS, BS), BF16),
    ]
    sem = pltpu.SemaphoreType.DMA

    sent = pl.pallas_call(
        first_kernel,
        out_shape=SENT,
        in_specs=[ANY] * 2,
        out_specs=[VM] * 4,
        scratch_shapes=[table, blocks, sem, sem],
        compiler_params=params(),
        name="first",
    )(pattern, factors)
    got = exchange(sent)
    zeroed = pl.pallas_call(
        zero_kernel,
        out_shape=jax.ShapeDtypeStruct(factors.shape, F32),
        out_specs=ANY,
        scratch_shapes=[pltpu.VMEM((64, factors.shape[1]), F32), sem],
        compiler_params=params(),
        cost_estimate=pl.CostEstimate(flops=0, bytes_accessed=factors.size * 4, transcendentals=0),
        name="zeros",
    )()
    *sent, state = pl.pallas_call(
        middle_kernel,
        out_shape=[*SENT, jax.ShapeDtypeStruct((SLOTS, BS, BS), F32)],
        in_specs=[ANY] * 8,
        out_specs=[VM] * 4 + [ANY],
        scratch_shapes=[table, blocks, halves, *operands, pltpu.SemaphoreType.DMA((5,))],
        compiler_params=params(),
        name="middle",
    )(pattern, factors, matrix, inverse, *got)
    got = exchange(sent)
    return pl.pallas_call(
        last_kernel,
        out_shape=jax.ShapeDtypeStruct(factors.shape, F32),
        in_specs=[ANY] * 10,
        out_specs=ANY,
        scratch_shapes=[table, table, blocks, halves, *operands, pltpu.SemaphoreType.DMA((6,))],
        input_output_aliases={9: 0},
        compiler_params=params(),
        name="last",
    )(pattern, dropped, matrix, inverse, state, *got, zeroed)


def solution(mesh):
    placed = (
        P("row", "col"),
        P("row", "col"),
        P("col", None, None),
        P("row", "col"),
        P("row", "col"),
    )
    return jax.shard_map(
        on_device, mesh=mesh, in_specs=placed, out_specs=P("row", "col"), check_vma=False
    )
```

```python
import functools

import jax
import jax.numpy as jnp
import numpy as np
from jax import lax
from jax.experimental import pallas as pl
from jax.experimental.pallas import tpu as pltpu
from jax.sharding import PartitionSpec as P

BS = 128
F32 = jnp.float32
BF16 = jnp.bfloat16

DIAG, X, OFF = 0, 4, 5
HELD = 9


def role():
    r, c = lax.axis_index("row"), lax.axis_index("col")
    odd = lax.rem(r, 2)
    home = lax.div(r, 2)
    late = r >= 8
    is_odd = odd == 1
    even = odd == 0
    is_d = c == home
    is_n = jnp.where(is_odd, c == home + 1, c == home - 1)
    is_f = jnp.where(late, c == home - 4, c == home + 4)
    lower = (is_d & is_odd) | (is_n & even) | (is_f & late)
    held = is_d | is_n | is_f
    return dict(
        even=even,
        top=r == 0,
        d=is_d,
        d_even=is_d & even,
        d_odd=is_d & is_odd,
        d_late=is_d & late,
        d_early=is_d & jnp.logical_not(late),
        n_even=is_n & even,
        n_odd=is_n & is_odd,
        f=is_f,
        f_late=is_f & late,
        f_early=is_f & jnp.logical_not(late),
        near=is_d | is_n,
        any=held,
        lower=lower,
        near_lower=lower & jnp.logical_not(is_f),
        upper=held & jnp.logical_not(lower),
        near_upper=held & jnp.logical_not(lower) & jnp.logical_not(is_f),
        first=4 * odd,
        off=jnp.where(is_f, 4 * odd, 4 * (1 - odd)),
        x_row=jnp.where(is_odd, jnp.where(is_d, 0, 3), jnp.where(is_d, 3, 0)),
        x_col=jnp.where(is_odd, jnp.where(is_d, 3, 0), jnp.where(is_d, 4, 7)),
    )


def spot(w, slot):
    if slot == X:
        return w["x_row"], w["x_col"]
    if slot < X:
        return slot, w["first"] + slot
    return slot - OFF, w["off"] + slot - OFF


def block(ref, i, c):
    return ref.at[pl.ds(pl.multiple_of(i * BS, BS), BS), pl.ds(pl.multiple_of(c * BS, BS), BS)]


def dot(a, b):
    return jnp.dot(a, b, preferred_element_type=F32)


class Copies:
    def __init__(self, sem):
        self.sem, self.todo = sem, []

    def add(self, when, src, dst):
        self.todo.append((when, src, dst))

    def run(self, start):
        i = 0
        while i < len(self.todo):
            when = self.todo[i][0]
            j = i
            while j < len(self.todo) and self.todo[j][0] is when:
                j += 1
            some = self.todo[i:j]

            def act(some=some):
                for _, src, dst in some:
                    copy = pltpu.make_async_copy(src, dst, self.sem)
                    copy.start() if start else copy.wait()

            if when is None:
                act()
            else:
                pl.when(when)(act)
            i = j


def member(table, place):
    return (table[place] == 1).astype(F32)


def cut_kernel(pattern, factors, sa, sb, sc, sd, held, table, sem, table_sem):
    w = role()

    @pl.when(w["any"])
    def _():
        get_table = pltpu.make_async_copy(pattern, table, table_sem)
        get_table.start()
        blocks = Copies(sem)
        for s in range(HELD):
            when = w["d"] if s < X else w["near"] if s == X else None
            blocks.add(when, block(factors, *spot(w, s)), held.at[s])
        blocks.run(True)
        get_table.wait()
        blocks.run(False)

        def masked(s):
            value = held[s] * member(table, spot(w, s))
            held[s] = value
            return value.astype(BF16)

        @pl.when(w["d"])
        def _():
            for j in range(4):
                value = masked(DIAG + j)
                sc[j] = value

                @pl.when(w["even"])
                def _():
                    sb[j] = value

                @pl.when(w["d_odd"])
                def _():
                    sa[j] = value

        @pl.when(w["f_early"])
        def _():
            for j in range(4):
                sd[j] = masked(OFF + j)

        @pl.when(w["f_late"])
        def _():
            for j in range(4):
                sc[j] = masked(OFF + j)

        @pl.when(w["d_even"] | w["n_odd"])
        def _():
            for j in range(4):
                sa[j] = masked(OFF + j)
            sa[4] = masked(X)

        @pl.when(w["n_even"])
        def _():
            for j in range(4):
                sb[j] = masked(OFF + j)
            sb[4] = masked(X)

        @pl.when(w["d_odd"])
        def _():
            for j in range(4):
                masked(OFF + j)
            masked(X)


def stage_kernel(pattern, dropped, factors, matrix, inverse, held,
                 out, base, base2, upper_b, a_low, left1, inv, keep,
                 zeros, f, a, done, table, drops, sems):
    w = role()
    zeros[...] = jnp.zeros_like(zeros)
    rows = zeros.shape[0]
    fill = Copies(sems.at[0])
    for k in range(out.shape[0] // rows):
        fill.add(None, zeros, out.at[pl.ds(k * rows, rows)])
    tables = Copies(sems.at[1])
    tables.add(None, pattern, table)
    tables.add(None, dropped, drops)
    blocks = Copies(sems.at[2])
    right = [(j, w["first"] + j + 1) for j in range(3)]
    left = [(j + 1, w["first"] + j) for j in range(3)]
    for k, place in enumerate(right + left):
        blocks.add(w["d"], block(factors, *place), f.at[k])
    for s in range(X):
        blocks.add(w["d"], block(matrix, *spot(w, s)), a.at[s])
    for k, place in enumerate(right + left):
        blocks.add(w["d"], block(matrix, *place), a.at[HELD + k])
    blocks.add(w["near"], block(matrix, *spot(w, X)), a.at[X])
    for s in range(OFF, HELD):
        blocks.add(None, block(matrix, *spot(w, s)), a.at[s])
    blocks.add(None, inverse, inv)

    @pl.when(w["any"])
    def _():
        tables.run(True)
        blocks.run(True)

    fill.run(True)

    @pl.when(w["any"])
    def _():
        tables.run(False)
        blocks.run(False)

        def kept(place):
            return (1 - drops[place]).astype(F32)

        def upper(old, a_block, place):
            m = member(table, place)
            a_block = a_block.astype(F32)
            one = old + (a_block - old) * m
            return one, (one + (a_block - one) * m) * kept(place)

        @pl.when(w["upper"])
        def _():
            for s in range(X, HELD):

                def act(s=s):
                    one, two = upper(held[s], a[s], spot(w, s))
                    upper_b[s - X] = one.astype(BF16)
                    done[s - X] = two

                act() if s > X else pl.when(w["near_upper"])(act)

        @pl.when(w["lower"])
        def _():
            for s in range(X, HELD):

                def act(s=s):
                    place = spot(w, s)
                    a_low[s - X] = (a[s].astype(F32) * member(table, place)).astype(BF16)
                    keep[s - X] = jnp.full(keep.shape[1:], kept(place))

                act() if s > X else pl.when(w["near_lower"])(act)

        @pl.when(w["d"])
        def _():
            base[0] = a[0].astype(F32)
            base2[0] = a[0].astype(F32)
            for j in range(3):
                old_u = f[j] * member(table, right[j])
                one_u, two_u = upper(old_u, a[HELD + j], right[j])
                done[5 + j] = two_u
                m = member(table, left[j])
                old = f[3 + j] * m
                old_b = old.astype(BF16)
                a_block = a[HELD + 3 + j].astype(F32) * m
                residual = a_block - dot(old_b, held[DIAG + j].astype(BF16)) * m
                one = old + dot(residual.astype(BF16), inv[w["first"] + j]) * m
                left1[j] = one
                a_low[5 + j] = a_block.astype(BF16)
                keep[5 + j] = jnp.full(keep.shape[1:], kept(left[j]))
                a_diag = a[j + 1].astype(F32)
                base[j + 1] = a_diag - dot(old_b, old_u.astype(BF16))
                base2[j + 1] = a_diag - dot(one.astype(BF16), one_u.astype(BF16))

    fill.run(False)
    finished = Copies(sems.at[3])
    for s in range(OFF, HELD):
        finished.add(w["upper"], done.at[s - X], block(out, *spot(w, s)))
    finished.add(w["near_upper"], done.at[0], block(out, *spot(w, X)))
    for j in range(3):
        finished.add(w["d"], done.at[5 + j], block(out, *right[j]))
    finished.run(True)
    finished.run(False)


def diagonal(w, sums, l_near, l_x, ra, rc, rd):
    def at(j, with_near, with_far):
        total = sums[j]
        if with_near:
            total = total - dot(l_near(j), ra[j])
        if with_near and j == 0:
            total = total - dot(l_x(), ra[4])
        if with_far:
            total = total - dot(rc[j], rd[j])
        return total

    return at


def lower_step(old, a_block, u, inv_block):
    residual = a_block.astype(F32) - dot(old.astype(BF16), u)
    return old + dot(residual.astype(BF16), inv_block)


def each_diagonal(w, emit, sums, own, rb, ra, rc, rd):
    for parity, l_near, l_x in (
        ("d_even", lambda j: rb[j], lambda: rb[4]),
        ("d_odd", lambda j: own[OFF + j].astype(BF16), lambda: own[X].astype(BF16)),
    ):
        at = diagonal(w, sums, l_near, l_x, ra, rc, rd)
        for near, far in ((False, False), (True, False), (True, True)):
            if not near and parity == "d_odd":
                continue
            when = w["d_late"] if far else w["d_early"] & (w["top"] != near)

            @pl.when(w[parity] & when)
            def _():
                for j in range(4):
                    emit(j, at(j, near, far))


def middle_kernel(held, base, upper_b, a_low, inv, ra, rb, rc, rd,
                  sa, sb, sc, sd, diag1, low1):
    w = role()

    def emit(j, total):
        old = held[DIAG + j]
        one = old + (total - old)
        diag1[j] = one
        value = one.astype(BF16)

        @pl.when(w["even"])
        def _():
            sb[j] = value

        @pl.when(w["d_odd"])
        def _():
            sa[j] = value

        @pl.when(w["d_early"])
        def _():
            sc[j] = value

    each_diagonal(w, emit, base, held, rb, ra, rc, rd)

    @pl.when(w["d_even"] | w["n_odd"])
    def _():
        for j in range(4):
            sa[j] = upper_b[1 + j]
        sa[4] = upper_b[0]

    @pl.when(w["f_early"])
    def _():
        for j in range(4):
            sd[j] = upper_b[1 + j]

    def lower(dst, u, j, s):
        one = lower_step(held[s], a_low[s - X], u[j], inv[w["off"] + j])
        low1[s - X] = one
        dst[s - OFF if s > X else 4] = one.astype(BF16)

    @pl.when(w["n_even"])
    def _():
        for j in range(4):
            lower(sb, ra, j, OFF + j)
        lower(sb, ra, 3, X)

    @pl.when(w["f_late"])
    def _():
        for j in range(4):
            lower(sc, rc, j, OFF + j)


def between_kernel(held, diag1, left1, a_low, inv, keep, rb, out_in, out, low1, done, sem):
    del out_in
    w = role()

    @pl.when(w["d"])
    def _():
        writes = Copies(sem)
        for j in range(3):
            u = diag1[j].astype(BF16)
            two = lower_step(left1[j], a_low[5 + j], u, inv[w["first"] + j])
            done[j] = two * keep[5 + j, 0:1, :]
            writes.add(None, done.at[j], block(out, j + 1, w["first"] + j))
        writes.run(True)

        @pl.when(w["d_odd"])
        def _():
            for j in range(4):
                low1[1 + j] = lower_step(held[OFF + j], a_low[1 + j], rb[j], inv[w["off"] + j])
            low1[0] = lower_step(held[X], a_low[0], rb[3], inv[w["off"] + 3])

        writes.run(False)


def last_kernel(diag1, base2, low1, low1_d, a_low, inv, keep, ra, rb, rc, rd, out_in,
                out, done, sem):
    del out_in
    w = role()
    writes = Copies(sem)
    for j in range(4):
        writes.add(w["d"], done.at[j], block(out, *spot(w, j)))
    for s in range(OFF, HELD):
        writes.add(w["lower"], done.at[s], block(out, *spot(w, s)))
    writes.add(w["near_lower"], done.at[X], block(out, *spot(w, X)))

    class Own:
        def __getitem__(self, s):
            return low1_d[s - X]

    def emit(j, total):
        old = diag1[j]
        done[DIAG + j] = old + (total - old)

    each_diagonal(w, emit, base2, Own(), rb, ra, rc, rd)

    def lower(old, u, j, s):
        two = lower_step(old[s - X], a_low[s - X], u[j], inv[w["off"] + j])
        done[s] = two * keep[s - X, 0:1, :]

    for name, old, u in (("d_odd", low1_d, rb), ("n_even", low1, ra), ("f_late", low1, rc)):

        @pl.when(w[name])
        def _():
            for j in range(4):
                lower(old, u, j, OFF + j)
            if name != "f_late":
                lower(old, u, 3, X)

    writes.run(True)
    writes.run(False)


def matched(cost):
    n = len(cost)
    u, v = np.zeros(n + 1), np.zeros(n + 1)
    owner = np.zeros(n + 1, int)
    for i in range(1, n + 1):
        owner[0], j0 = i, 0
        best = np.full(n + 1, np.inf)
        back = np.zeros(n + 1, int)
        used = np.zeros(n + 1, bool)
        while owner[j0]:
            used[j0] = True
            i0 = owner[j0]
            slack = cost[i0 - 1] - u[i0] - v[1:]
            better = ~used[1:] & (slack < best[1:])
            best[1:][better] = slack[better]
            back[1:][better] = j0
            j1 = int(np.argmin(np.where(used, np.inf, best)))
            delta = best[j1]
            u[owner[used]] += delta
            v[used] -= delta
            best[~used] -= delta
            j0 = j1
        while j0:
            owner[j0] = owner[back[j0]]
            j0 = back[j0]
    return {int(owner[j]) - 1: j - 1 for j in range(1, n + 1)}


def distance(a, b):
    def chip(i):
        r, c = divmod(i, 8)
        return ((r // 2) % 2) * 2 + c % 2, c // 2, r // 4

    return sum(min(abs(p - q), 4 - abs(p - q)) for p, q in zip(chip(a), chip(b)))


def whole(pairs, busy):
    sends, takes = {a for a, _ in pairs}, {b for _, b in pairs}
    free_a = [i for i in range(128) if i not in sends]
    free_b = [i for i in range(128) if i not in takes]

    def price(a, b):
        if a == b:
            return 1e6
        far = distance(a, b)
        return (2 + far if far else 1) ** 2 * sum(10 if i in busy else 1 for i in (a, b))

    pick = matched(np.array([[price(a, b) for b in free_b] for a in free_a], float))
    return list(pairs) + [(a, free_b[pick[i]]) for i, a in enumerate(free_a)]


def routes():
    def at(r, c):
        return r * 8 + c

    diag = [at(r, r // 2) for r in range(16)]
    near = {r: at(r, r // 2 + (1 if r % 2 else -1)) for r in range(1, 15)}
    far = [at(r, r // 2 + (4 if r < 8 else -4)) for r in range(16)]
    busy = {*diag, *near.values(), *far}
    pair = [(diag[r], diag[r + 1]) for r in range(0, 16, 2)]
    a = pair + [(diag[r], near[r + 1]) for r in range(1, 14, 2)]
    a += [(near[r], diag[r + 1]) for r in range(1, 14, 2)]
    b = pair + [(near[r], diag[r]) for r in range(2, 15, 2)]
    c, d = [], []
    for r in range(8):
        ring = [diag[r], far[r + 8], diag[r + 8], far[r]]
        c += list(zip(ring, ring[1:] + ring[:1]))
        d += [(far[r], diag[r + 8]), (diag[r + 8], far[r])]
    return [whole(x, busy) for x in (a, b, c, d)]


def exchange(buffers):
    out = [None] * 4
    for k in ORDER:
        out[k] = lax.ppermute(buffers[k], ("row", "col"), ROUTES[k])
    return out


ROUTES = routes()
ORDER = (1, 0, 2, 3)
ANY = pl.BlockSpec(memory_space=pl.ANY)
VM = pl.BlockSpec(memory_space=pltpu.VMEM)
MIB = 1 << 20


def wide(n):
    return jax.ShapeDtypeStruct((n, BS, BS), F32)


def half(n):
    return jax.ShapeDtypeStruct((n, BS, BS), BF16)


SENT = [half(5), half(5), half(4), half(4)]


def call(kernel, name, out_shape, in_specs, out_specs, scratch, aliases=None, cost=None):
    return pl.pallas_call(
        kernel,
        out_shape=out_shape,
        in_specs=in_specs,
        out_specs=out_specs,
        scratch_shapes=scratch,
        input_output_aliases=aliases or {},
        compiler_params=pltpu.CompilerParams(vmem_limit_bytes=20 * MIB),
        cost_estimate=cost and pl.CostEstimate(flops=cost[0], bytes_accessed=cost[1], transcendentals=0),
        name=name,
    )


def on_device(matrix, factors, inverse, pattern, dropped):
    matrix, factors, inverse, pattern, dropped = (
        pltpu.with_memory_space_constraint(x, pltpu.HBM)
        for x in (matrix, factors, inverse, pattern, dropped)
    )
    table = pltpu.SMEM(pattern.shape, jnp.int32)
    sem = pltpu.SemaphoreType.DMA
    whole_out = jax.ShapeDtypeStruct(factors.shape, F32)

    *sent, held = call(
        cut_kernel, "cut", [*SENT, wide(HELD)], [ANY] * 2, [VM] * 5, [table, sem, sem],
    )(pattern, factors)
    got = exchange(sent)
    out, base, base2, upper_b, a_low, left1, inv, keep = call(
        stage_kernel,
        "stage",
        [whole_out, wide(4), wide(4), half(5), half(8), wide(3), half(inverse.shape[0]),
         jax.ShapeDtypeStruct((8, 8, BS), F32)],
        [ANY] * 5 + [VM],
        [ANY] + [VM] * 7,
        [pltpu.VMEM((64, factors.shape[1]), F32), pltpu.VMEM((6, BS, BS), F32),
         pltpu.VMEM((15, BS, BS), BF16), pltpu.VMEM((8, BS, BS), F32), table, table, sem((4,))],
        cost=(60_000_000, 6_000_000),
    )(pattern, dropped, factors, matrix, inverse, held)
    *sent, diag1, low1 = call(
        middle_kernel, "middle", [*SENT, wide(4), wide(5)], [VM] * 9, [VM] * 6, [],
    )(held, base, upper_b, a_low, inv, *got)
    got2 = exchange(sent)
    out, low1_d = call(
        between_kernel,
        "between",
        [whole_out, wide(5)],
        [VM] * 7 + [ANY],
        [ANY, VM],
        [pltpu.VMEM((3, BS, BS), F32), sem],
        aliases={7: 0},
        cost=(60_000_000, 2_000_000),
    )(held, diag1, left1, a_low, inv, keep, got[1], out)
    return call(
        last_kernel,
        "last",
        whole_out,
        [VM] * 11 + [ANY],
        ANY,
        [pltpu.VMEM((HELD, BS, BS), F32), sem],
        aliases={11: 0},
    )(diag1, base2, low1, low1_d, a_low, inv, keep, *got2, out)


def solution(mesh):
    placed = (
        P("row", "col"),
        P("row", "col"),
        P("col", None, None),
        P("row", "col"),
        P("row", "col"),
    )
    return jax.shard_map(
        on_device, mesh=mesh, in_specs=placed, out_specs=P("row", "col"), check_vma=False
    )
```

```python
import functools

import jax
import jax.numpy as jnp
import numpy as np
from jax import lax
from jax.experimental import pallas as pl
from jax.experimental.pallas import tpu as pltpu
from jax.sharding import PartitionSpec as P

BS = 128
F32 = jnp.float32
BF16 = jnp.bfloat16

DIAG, X, OFF = 0, 4, 5
HELD = 9


def role():
    r, c = lax.axis_index("row"), lax.axis_index("col")
    odd = lax.rem(r, 2)
    home = lax.div(r, 2)
    late = r >= 8
    is_odd = odd == 1
    even = odd == 0
    is_d = c == home
    is_n = jnp.where(is_odd, c == home + 1, c == home - 1)
    is_f = jnp.where(late, c == home - 4, c == home + 4)
    lower = (is_d & is_odd) | (is_n & even) | (is_f & late)
    held = is_d | is_n | is_f
    return dict(
        even=even,
        top=r == 0,
        d=is_d,
        d_even=is_d & even,
        d_odd=is_d & is_odd,
        d_late=is_d & late,
        d_early=is_d & jnp.logical_not(late),
        n_even=is_n & even,
        n_odd=is_n & is_odd,
        f=is_f,
        f_late=is_f & late,
        f_early=is_f & jnp.logical_not(late),
        near=is_d | is_n,
        any=held,
        lower=lower,
        near_lower=lower & jnp.logical_not(is_f),
        upper=held & jnp.logical_not(lower),
        near_upper=held & jnp.logical_not(lower) & jnp.logical_not(is_f),
        first=4 * odd,
        off=jnp.where(is_f, 4 * odd, 4 * (1 - odd)),
        x_row=jnp.where(is_odd, jnp.where(is_d, 0, 3), jnp.where(is_d, 3, 0)),
        x_col=jnp.where(is_odd, jnp.where(is_d, 3, 0), jnp.where(is_d, 4, 7)),
    )


def spot(w, slot):
    if slot == X:
        return w["x_row"], w["x_col"]
    if slot < X:
        return slot, w["first"] + slot
    return slot - OFF, w["off"] + slot - OFF


def block(ref, i, c):
    return ref.at[pl.ds(pl.multiple_of(i * BS, BS), BS), pl.ds(pl.multiple_of(c * BS, BS), BS)]


def dot(a, b):
    return jnp.dot(a, b, preferred_element_type=F32)


class Copies:
    def __init__(self, sem):
        self.sem, self.todo = sem, []

    def add(self, when, src, dst):
        self.todo.append((when, src, dst))

    def run(self, start):
        i = 0
        while i < len(self.todo):
            when = self.todo[i][0]
            j = i
            while j < len(self.todo) and self.todo[j][0] is when:
                j += 1
            some = self.todo[i:j]

            def act(some=some):
                for _, src, dst in some:
                    copy = pltpu.make_async_copy(src, dst, self.sem)
                    copy.start() if start else copy.wait()

            if when is None:
                act()
            else:
                pl.when(when)(act)
            i = j


def member(table, place):
    return (table[place] == 1).astype(F32)


def cut_kernel(plan, pattern, factors, sa, sb, sc, sd, held, table, sem, table_sem):
    w = role()
    s_near, s_low, s_up = plan.sends(sa, sb, sc, sd)

    @pl.when(w["any"])
    def _():
        get_table = pltpu.make_async_copy(pattern, table, table_sem)
        get_table.start()
        blocks = Copies(sem)
        for s in range(HELD):
            when = w["d"] if s < X else w["near"] if s == X else None
            blocks.add(when, block(factors, *spot(w, s)), held.at[s])
        blocks.run(True)
        get_table.wait()
        blocks.run(False)

        def masked(s):
            value = held[s] * member(table, spot(w, s))
            held[s] = value
            return value.astype(BF16)

        @pl.when(w["d"])
        def _():
            for j in range(4):
                value = masked(DIAG + j)
                sc[j] = value

                @pl.when(w["even"])
                def _():
                    sb[j] = value

                @pl.when(w["d_odd"])
                def _():
                    s_near[j] = value

        @pl.when(w["f_early"])
        def _():
            for j in range(4):
                s_up[j] = masked(OFF + j)

        @pl.when(w["f_late"])
        def _():
            for j in range(4):
                s_low[j] = masked(OFF + j)

        @pl.when(w["d_even"] | w["n_odd"])
        def _():
            for j in range(4):
                sa[j] = masked(OFF + j)
            sa[4] = masked(X)

        @pl.when(w["n_even"])
        def _():
            for j in range(4):
                sb[j] = masked(OFF + j)
            sb[4] = masked(X)

        @pl.when(w["d_odd"])
        def _():
            for j in range(4):
                masked(OFF + j)
            masked(X)


def stage_kernel(pattern, dropped, factors, matrix, inverse, held,
                 out, base, base2, upper_b, upper_f, a_low, left1, inv, keep,
                 zeros, f, a, done, table, drops, sems):
    w = role()
    zeros[...] = jnp.zeros_like(zeros)
    rows = zeros.shape[0]
    fill = Copies(sems.at[0])
    for k in range(out.shape[0] // rows):
        fill.add(None, zeros, out.at[pl.ds(k * rows, rows)])
    tables = Copies(sems.at[1])
    tables.add(None, pattern, table)
    tables.add(None, dropped, drops)
    blocks = Copies(sems.at[2])
    right = [(j, w["first"] + j + 1) for j in range(3)]
    left = [(j + 1, w["first"] + j) for j in range(3)]
    for k, place in enumerate(right + left):
        blocks.add(w["d"], block(factors, *place), f.at[k])
    for s in range(X):
        blocks.add(w["d"], block(matrix, *spot(w, s)), a.at[s])
    for k, place in enumerate(right + left):
        blocks.add(w["d"], block(matrix, *place), a.at[HELD + k])
    blocks.add(w["near"], block(matrix, *spot(w, X)), a.at[X])
    for s in range(OFF, HELD):
        blocks.add(None, block(matrix, *spot(w, s)), a.at[s])
    blocks.add(None, inverse, inv)

    @pl.when(w["any"])
    def _():
        tables.run(True)
        blocks.run(True)

    fill.run(True)

    @pl.when(w["any"])
    def _():
        tables.run(False)
        blocks.run(False)

        def kept(place):
            return (1 - drops[place]).astype(F32)

        def upper(old, a_block, place):
            m = member(table, place)
            a_block = a_block.astype(F32)
            one = old + (a_block - old) * m
            return one, (one + (a_block - one) * m) * kept(place)

        @pl.when(w["upper"])
        def _():
            for s in range(X, HELD):

                def act(s=s):
                    one, two = upper(held[s], a[s], spot(w, s))
                    one = one.astype(BF16)
                    upper_b[s - OFF if s > X else 4] = one
                    if s > X:
                        upper_f[s - OFF] = one
                    done[s - X] = two

                act() if s > X else pl.when(w["near_upper"])(act)

        @pl.when(w["lower"])
        def _():
            for s in range(X, HELD):

                def act(s=s):
                    place = spot(w, s)
                    a_low[s - X] = (a[s].astype(F32) * member(table, place)).astype(BF16)
                    keep[s - X] = jnp.full(keep.shape[1:], kept(place))

                act() if s > X else pl.when(w["near_lower"])(act)

        @pl.when(w["d"])
        def _():
            base[0] = a[0].astype(F32)
            base2[0] = a[0].astype(F32)
            for j in range(3):
                old_u = f[j] * member(table, right[j])
                one_u, two_u = upper(old_u, a[HELD + j], right[j])
                done[5 + j] = two_u
                m = member(table, left[j])
                old = f[3 + j] * m
                old_b = old.astype(BF16)
                a_block = a[HELD + 3 + j].astype(F32) * m
                residual = a_block - dot(old_b, held[DIAG + j].astype(BF16)) * m
                one = old + dot(residual.astype(BF16), inv[w["first"] + j]) * m
                left1[j] = one
                a_low[5 + j] = a_block.astype(BF16)
                keep[5 + j] = jnp.full(keep.shape[1:], kept(left[j]))
                a_diag = a[j + 1].astype(F32)
                base[j + 1] = a_diag - dot(old_b, old_u.astype(BF16))
                base2[j + 1] = a_diag - dot(one.astype(BF16), one_u.astype(BF16))

    fill.run(False)
    finished = Copies(sems.at[3])
    for s in range(OFF, HELD):
        finished.add(w["upper"], done.at[s - X], block(out, *spot(w, s)))
    finished.add(w["near_upper"], done.at[0], block(out, *spot(w, X)))
    for j in range(3):
        finished.add(w["d"], done.at[5 + j], block(out, *right[j]))
    finished.run(True)
    finished.run(False)


def diagonal(w, sums, l_near, l_x, ra, rc, rd):
    def at(j, with_near, with_far):
        total = sums[j]
        if with_near:
            total = total - dot(l_near(j), ra[j])
        if with_near and j == 0:
            total = total - dot(l_x(), ra[4])
        if with_far:
            total = total - dot(rc[j], rd[j])
        return total

    return at


def lower_step(old, a_block, u, inv_block):
    residual = a_block.astype(F32) - dot(old.astype(BF16), u)
    return old + dot(residual.astype(BF16), inv_block)


def each_diagonal(w, emit, sums, own, rb, ra, rc, rd):
    for parity, l_near, l_x in (
        ("d_even", lambda j: rb[j], lambda: rb[4]),
        ("d_odd", lambda j: own[OFF + j].astype(BF16), lambda: own[X].astype(BF16)),
    ):
        at = diagonal(w, sums, l_near, l_x, ra, rc, rd)
        for near, far in ((False, False), (True, False), (True, True)):
            if not near and parity == "d_odd":
                continue
            when = w["d_late"] if far else w["d_early"] & (w["top"] != near)

            @pl.when(w[parity] & when)
            def _():
                for j in range(4):
                    emit(j, at(j, near, far))


def middle_kernel(plan, held, base, a_low, inv, ra, rb, rc, rd, sb, sc, diag1, low1):
    w = role()
    r_near, r_low, r_up = plan.sends(ra, rb, rc, rd)

    def emit(j, total):
        old = held[DIAG + j]
        one = old + (total - old)
        diag1[j] = one
        value = one.astype(BF16)
        sb[j] = value

        @pl.when(w["d_early"])
        def _():
            sc[j] = value

    each_diagonal(w, emit, base, held, rb, ra, r_low, r_up)

    def lower(dst, u, j, s):
        one = lower_step(held[s], a_low[s - X], u[j], inv[w["off"] + j])
        low1[s - X] = one
        dst[s - OFF if s > X else 4] = one.astype(BF16)

    @pl.when(w["n_even"])
    def _():
        for j in range(4):
            lower(sb, r_near, j, OFF + j)
        lower(sb, r_near, 3, X)

    @pl.when(w["f_late"])
    def _():
        for j in range(4):
            lower(sc, rc, j, OFF + j)


def between_kernel(held, diag1, left1, a_low, inv, keep, rb, out_in, out, low1, done, sem):
    del out_in
    w = role()

    @pl.when(w["d"])
    def _():
        writes = Copies(sem)
        for j in range(3):
            u = diag1[j].astype(BF16)
            two = lower_step(left1[j], a_low[5 + j], u, inv[w["first"] + j])
            done[j] = two * keep[5 + j, 0:1, :]
            writes.add(None, done.at[j], block(out, j + 1, w["first"] + j))
        writes.run(True)

        @pl.when(w["d_odd"])
        def _():
            for j in range(4):
                low1[1 + j] = lower_step(held[OFF + j], a_low[1 + j], rb[j], inv[w["off"] + j])
            low1[0] = lower_step(held[X], a_low[0], rb[3], inv[w["off"] + 3])

        writes.run(False)


def last_kernel(plan, diag1, base2, low1, low1_d, a_low, inv, keep, ra, rb, rc, rd, out_in,
                out, done, sem):
    del out_in
    w = role()
    r_near, r_low, r_up = plan.sends(ra, rb, rc, rd)
    writes = Copies(sem)
    for j in range(4):
        writes.add(w["d"], done.at[j], block(out, *spot(w, j)))
    for s in range(OFF, HELD):
        writes.add(w["lower"], done.at[s], block(out, *spot(w, s)))
    writes.add(w["near_lower"], done.at[X], block(out, *spot(w, X)))

    class Own:
        def __getitem__(self, s):
            return low1_d[s - X]

    def emit(j, total):
        old = diag1[j]
        done[DIAG + j] = old + (total - old)

    each_diagonal(w, emit, base2, Own(), rb, ra, r_low, r_up)

    def lower(old, u, j, s):
        two = lower_step(old[s - X], a_low[s - X], u[j], inv[w["off"] + j])
        done[s] = two * keep[s - X, 0:1, :]

    for name, old, u in (("d_odd", low1_d, rb), ("n_even", low1, r_near), ("f_late", low1, rc)):

        @pl.when(w[name])
        def _():
            for j in range(4):
                lower(old, u, j, OFF + j)
            if name != "f_late":
                lower(old, u, 3, X)

    writes.run(True)
    writes.run(False)


def matched(cost):
    n = len(cost)
    u, v = np.zeros(n + 1), np.zeros(n + 1)
    owner = np.zeros(n + 1, int)
    for i in range(1, n + 1):
        owner[0], j0 = i, 0
        best = np.full(n + 1, np.inf)
        back = np.zeros(n + 1, int)
        used = np.zeros(n + 1, bool)
        while owner[j0]:
            used[j0] = True
            i0 = owner[j0]
            slack = cost[i0 - 1] - u[i0] - v[1:]
            better = ~used[1:] & (slack < best[1:])
            best[1:][better] = slack[better]
            back[1:][better] = j0
            j1 = int(np.argmin(np.where(used, np.inf, best)))
            delta = best[j1]
            u[owner[used]] += delta
            v[used] -= delta
            best[~used] -= delta
            j0 = j1
        while j0:
            owner[j0] = owner[back[j0]]
            j0 = back[j0]
    return {int(owner[j]) - 1: j - 1 for j in range(1, n + 1)}


def distance(a, b):
    def chip(i):
        r, c = divmod(i, 8)
        return ((r // 2) % 2) * 2 + c % 2, c // 2, r // 4

    return sum(min(abs(p - q), 4 - abs(p - q)) for p, q in zip(chip(a), chip(b)))


def whole(pairs, busy):
    sends, takes = {a for a, _ in pairs}, {b for _, b in pairs}
    free_a = [i for i in range(128) if i not in sends]
    free_b = [i for i in range(128) if i not in takes]

    def price(a, b):
        if a == b:
            return 1e6
        far = distance(a, b)
        return (2 + far if far else 1) ** 2 * sum(10 if i in busy else 1 for i in (a, b))

    pick = matched(np.array([[price(a, b) for b in free_b] for a in free_a], float))
    return list(pairs) + [(a, free_b[pick[i]]) for i, a in enumerate(free_a)]


class Plan:
    def __init__(self, near, far_low, order, routes=None):
        self.near, self.far_low, self.order = near, far_low, order
        self.routes = routes

    def sends(self, *bufs):
        return bufs[self.near], bufs[self.far_low], bufs[5 - self.far_low]

    def needed(self):
        def at(r, c):
            return r * 8 + c

        diag = [at(r, r // 2) for r in range(16)]
        near = {r: at(r, r // 2 + (1 if r % 2 else -1)) for r in range(1, 15)}
        far = [at(r, r // 2 + (4 if r < 8 else -4)) for r in range(16)]
        pair = [(diag[r], diag[r + 1]) for r in range(0, 16, 2)]
        out = [list(pair), list(pair), [], []]
        out[0] += [(near[r], diag[r + 1]) for r in range(1, 14, 2)]
        out[1] += [(near[r], diag[r]) for r in range(2, 15, 2)]
        out[self.near] += [(diag[r], near[r + 1]) for r in range(1, 14, 2)]
        out[2] += [(diag[r], far[r + 8]) for r in range(8)]
        out[self.far_low] += [(far[r], diag[r]) for r in range(8, 16)]
        out[5 - self.far_low] += [(far[r], diag[r + 8]) for r in range(8)]
        return out, {*diag, *near.values(), *far}

    def full(self):
        needed, busy = self.needed()
        return self.routes or [whole(x, busy) for x in needed]


def exchange(plan, buffers):
    out = [None] * 4
    routes = plan.full()
    for k in plan.order:
        out[k] = lax.ppermute(buffers[k], ("row", "col"), routes[k])
    return out


PLANS = [Plan(0, 2, (1, 0, 2, 3)), Plan(1, 2, (0, 3, 1, 2))]
ANY = pl.BlockSpec(memory_space=pl.ANY)
VM = pl.BlockSpec(memory_space=pltpu.VMEM)
MIB = 1 << 20


def wide(n):
    return jax.ShapeDtypeStruct((n, BS, BS), F32)


def half(n):
    return jax.ShapeDtypeStruct((n, BS, BS), BF16)


def sent_shapes(plan):
    rows = [None] * 4
    for place, k in enumerate(plan.order):
        rows[k] = 5 if any(j < 2 for j in plan.order[place:]) else 4
    return [half(n) for n in rows]


def call(kernel, name, out_shape, in_specs, out_specs, scratch, aliases=None, cost=None):
    return pl.pallas_call(
        kernel,
        out_shape=out_shape,
        in_specs=in_specs,
        out_specs=out_specs,
        scratch_shapes=scratch,
        input_output_aliases=aliases or {},
        compiler_params=pltpu.CompilerParams(vmem_limit_bytes=20 * MIB),
        cost_estimate=cost and pl.CostEstimate(flops=cost[0], bytes_accessed=cost[1], transcendentals=0),
        name=name,
    )


def on_device(matrix, factors, inverse, pattern, dropped):
    matrix, factors, inverse, pattern, dropped = (
        pltpu.with_memory_space_constraint(x, pltpu.HBM)
        for x in (matrix, factors, inverse, pattern, dropped)
    )
    table = pltpu.SMEM(pattern.shape, jnp.int32)
    sem = pltpu.SemaphoreType.DMA
    whole_out = jax.ShapeDtypeStruct(factors.shape, F32)

    plan, next_plan = PLANS
    *sent, held = call(
        functools.partial(cut_kernel, plan), "cut", [*sent_shapes(plan), wide(HELD)],
        [ANY] * 2, [VM] * 5, [table, sem, sem],
    )(pattern, factors)
    got = exchange(plan, sent)
    out, base, base2, upper_b, upper_f, a_low, left1, inv, keep = call(
        stage_kernel,
        "stage",
        [whole_out, wide(4), wide(4), half(5), half(5), half(8), wide(3), half(inverse.shape[0]),
         jax.ShapeDtypeStruct((8, 8, BS), F32)],
        [ANY] * 5 + [VM],
        [ANY] + [VM] * 8,
        [pltpu.VMEM((64, factors.shape[1]), F32), pltpu.VMEM((6, BS, BS), F32),
         pltpu.VMEM((15, BS, BS), BF16), pltpu.VMEM((8, BS, BS), F32), table, table, sem((4,))],
        cost=(60_000_000, 6_000_000),
    )(pattern, dropped, factors, matrix, inverse, held)
    sent_b, sent_c, diag1, low1 = call(
        functools.partial(middle_kernel, plan), "middle",
        [half(5), half(4), wide(4), wide(5)], [VM] * 8, [VM] * 4, [],
    )(held, base, a_low, inv, *got)
    got2 = exchange(next_plan, (upper_b, sent_b, sent_c, upper_f))
    out, low1_d = call(
        between_kernel,
        "between",
        [whole_out, wide(5)],
        [VM] * 7 + [ANY],
        [ANY, VM],
        [pltpu.VMEM((3, BS, BS), F32), sem],
        aliases={7: 0},
        cost=(60_000_000, 2_000_000),
    )(held, diag1, left1, a_low, inv, keep, got[1], out)
    return call(
        functools.partial(last_kernel, next_plan),
        "last",
        whole_out,
        [VM] * 11 + [ANY],
        ANY,
        [pltpu.VMEM((HELD, BS, BS), F32), sem],
        aliases={11: 0},
    )(diag1, base2, low1, low1_d, a_low, inv, keep, *got2, out)


def solution(mesh):
    placed = (
        P("row", "col"),
        P("row", "col"),
        P("col", None, None),
        P("row", "col"),
        P("row", "col"),
    )
    return jax.shard_map(
        on_device, mesh=mesh, in_specs=placed, out_specs=P("row", "col"), check_vma=False
    )
```

```python
import functools

import jax
import jax.numpy as jnp
from jax import lax
from jax.experimental import pallas as pl
from jax.experimental.pallas import tpu as pltpu
from jax.sharding import PartitionSpec as P

BS = 128
F32 = jnp.float32
BF16 = jnp.bfloat16

DIAG, X, OFF = 0, 4, 5
HELD = 9


def role():
    r, c = lax.axis_index("row"), lax.axis_index("col")
    odd = lax.rem(r, 2)
    home = lax.div(r, 2)
    late = r >= 8
    is_odd = odd == 1
    even = odd == 0
    is_d = c == home
    is_n = jnp.where(is_odd, c == home + 1, c == home - 1)
    is_f = jnp.where(late, c == home - 4, c == home + 4)
    lower = (is_d & is_odd) | (is_n & even) | (is_f & late)
    held = is_d | is_n | is_f
    return dict(
        even=even,
        top=r == 0,
        d=is_d,
        d_even=is_d & even,
        d_odd=is_d & is_odd,
        d_late=is_d & late,
        d_early=is_d & jnp.logical_not(late),
        n_even=is_n & even,
        n_odd=is_n & is_odd,
        f=is_f,
        f_late=is_f & late,
        f_early=is_f & jnp.logical_not(late),
        near=is_d | is_n,
        any=held,
        lower=lower,
        near_lower=lower & jnp.logical_not(is_f),
        upper=held & jnp.logical_not(lower),
        near_upper=held & jnp.logical_not(lower) & jnp.logical_not(is_f),
        first=4 * odd,
        off=jnp.where(is_f, 4 * odd, 4 * (1 - odd)),
        x_row=jnp.where(is_odd, jnp.where(is_d, 0, 3), jnp.where(is_d, 3, 0)),
        x_col=jnp.where(is_odd, jnp.where(is_d, 3, 0), jnp.where(is_d, 4, 7)),
    )


def spot(w, slot):
    if slot == X:
        return w["x_row"], w["x_col"]
    if slot < X:
        return slot, w["first"] + slot
    return slot - OFF, w["off"] + slot - OFF


def block(ref, i, c):
    return ref.at[pl.ds(pl.multiple_of(i * BS, BS), BS), pl.ds(pl.multiple_of(c * BS, BS), BS)]


def dot(a, b):
    return jnp.dot(a, b, preferred_element_type=F32)


class Copies:
    def __init__(self, sem):
        self.sem, self.todo = sem, []

    def add(self, when, src, dst):
        self.todo.append((when, src, dst))

    def run(self, start):
        i = 0
        while i < len(self.todo):
            when = self.todo[i][0]
            j = i
            while j < len(self.todo) and self.todo[j][0] is when:
                j += 1
            some = self.todo[i:j]

            def act(some=some):
                for _, src, dst in some:
                    copy = pltpu.make_async_copy(src, dst, self.sem)
                    copy.start() if start else copy.wait()

            if when is None:
                act()
            else:
                pl.when(when)(act)
            i = j


def member(table, place):
    return (table[place] == 1).astype(F32)


def cut_kernel(pattern, factors, sa, sb, sc, sd, held, table, sem, table_sem):
    w = role()

    @pl.when(w["any"])
    def _():
        get_table = pltpu.make_async_copy(pattern, table, table_sem)
        get_table.start()
        blocks = Copies(sem)
        for s in range(HELD):
            when = w["d"] if s < X else w["near"] if s == X else None
            blocks.add(when, block(factors, *spot(w, s)), held.at[s])
        blocks.run(True)
        get_table.wait()
        blocks.run(False)

        def masked(s):
            value = held[s] * member(table, spot(w, s))
            held[s] = value
            return value.astype(BF16)

        @pl.when(w["d"])
        def _():
            for j in range(4):
                value = masked(DIAG + j)
                sc[j] = value

                @pl.when(w["even"])
                def _():
                    sb[j] = value

                @pl.when(w["d_odd"])
                def _():
                    sa[j] = value

        @pl.when(w["f_early"])
        def _():
            for j in range(4):
                sd[j] = masked(OFF + j)

        @pl.when(w["f_late"])
        def _():
            for j in range(4):
                sc[j] = masked(OFF + j)

        @pl.when(w["d_even"] | w["n_odd"])
        def _():
            for j in range(4):
                sa[j] = masked(OFF + j)
            sa[4] = masked(X)

        @pl.when(w["n_even"])
        def _():
            for j in range(4):
                sb[j] = masked(OFF + j)
            sb[4] = masked(X)

        @pl.when(w["d_odd"])
        def _():
            for j in range(4):
                masked(OFF + j)
            masked(X)


def kept(drops, place):
    return (1 - drops[place]).astype(F32)


def upper(table, drops, old, a_block, place):
    m = member(table, place)
    a_block = a_block.astype(F32)
    one = old + (a_block - old) * m
    return one, (one + (a_block - one) * m) * kept(drops, place)


def upper_kernel(pattern, dropped, matrix, held, upper_b, upper_f, done, a, table, drops, sems):
    w = role()

    @pl.when(w["upper"])
    def _():
        loads = Copies(sems.at[0])
        loads.add(None, pattern, table)
        loads.add(None, dropped, drops)
        blocks = Copies(sems.at[1])
        for s in range(OFF, HELD):
            blocks.add(None, block(matrix, *spot(w, s)), a.at[s - X])
        blocks.add(w["near_upper"], block(matrix, *spot(w, X)), a.at[0])
        loads.run(True)
        blocks.run(True)
        loads.run(False)
        blocks.run(False)
        for s in range(X, HELD):

            def act(s=s):
                one, done[s - X] = upper(table, drops, held[s], a[s - X], spot(w, s))
                one = one.astype(BF16)
                upper_b[s - OFF if s > X else 4] = one
                if s > X:
                    upper_f[s - OFF] = one

            act() if s > X else pl.when(w["near_upper"])(act)


def right_of(w):
    return [(j, w["first"] + j + 1) for j in range(3)]


def stage_kernel(pattern, dropped, factors, matrix, inverse, held,
                 base, base2, a_low, left1, inv, keep, done,
                 f, a, table, drops, sems):
    w = role()
    tables = Copies(sems.at[1])
    tables.add(None, pattern, table)
    tables.add(None, dropped, drops)
    blocks = Copies(sems.at[2])
    right = right_of(w)
    left = [(j + 1, w["first"] + j) for j in range(3)]
    for k, place in enumerate(right + left):
        blocks.add(w["d"], block(factors, *place), f.at[k])
    for s in range(X):
        blocks.add(w["d"], block(matrix, *spot(w, s)), a.at[s])
    for k, place in enumerate(right + left):
        blocks.add(w["d"], block(matrix, *place), a.at[HELD + k])
    blocks.add(w["near_lower"], block(matrix, *spot(w, X)), a.at[X])
    for s in range(OFF, HELD):
        blocks.add(w["lower"], block(matrix, *spot(w, s)), a.at[s])
    blocks.add(None, inverse, inv)

    @pl.when(w["any"])
    def _():
        tables.run(True)
        blocks.run(True)
        tables.run(False)
        blocks.run(False)

        @pl.when(w["lower"])
        def _():
            for s in range(X, HELD):

                def act(s=s):
                    place = spot(w, s)
                    a_low[s - X] = (a[s].astype(F32) * member(table, place)).astype(BF16)
                    keep[s - X] = jnp.full(keep.shape[1:], kept(drops, place))

                act() if s > X else pl.when(w["near_lower"])(act)

        @pl.when(w["d"])
        def _():
            base[0] = a[0].astype(F32)
            base2[0] = a[0].astype(F32)
            for j in range(3):
                old_u = f[j] * member(table, right[j])
                one_u, done[j] = upper(table, drops, old_u, a[HELD + j], right[j])
                m = member(table, left[j])
                old = f[3 + j] * m
                old_b = old.astype(BF16)
                a_block = a[HELD + 3 + j].astype(F32) * m
                residual = a_block - dot(old_b, held[DIAG + j].astype(BF16)) * m
                one = old + dot(residual.astype(BF16), inv[w["first"] + j]) * m
                left1[j] = one
                a_low[5 + j] = a_block.astype(BF16)
                keep[5 + j] = jnp.full(keep.shape[1:], kept(drops, left[j]))
                a_diag = a[j + 1].astype(F32)
                base[j + 1] = a_diag - dot(old_b, old_u.astype(BF16))
                base2[j + 1] = a_diag - dot(one.astype(BF16), one_u.astype(BF16))


def diagonal(w, sums, l_near, l_x, ra, rc, rd):
    def at(j, with_near, with_far):
        total = sums[j]
        if with_near:
            total = total - dot(l_near(j), ra[j])
        if with_near and j == 0:
            total = total - dot(l_x(), ra[4])
        if with_far:
            total = total - dot(rc[j], rd[j])
        return total

    return at


def lower_step(old, a_block, u, inv_block):
    residual = a_block.astype(F32) - dot(old.astype(BF16), u)
    return old + dot(residual.astype(BF16), inv_block)


def each_diagonal(w, late, emit, sums, own, rb, ra, rc, rd):
    for parity, l_near, l_x in (
        ("d_even", lambda j: rb[j], lambda: rb[4]),
        ("d_odd", lambda j: own[OFF + j].astype(BF16), lambda: own[X].astype(BF16)),
    ):
        at = diagonal(w, sums, l_near, l_x, ra, rc, rd)
        for near in (True,) if late or parity == "d_odd" else (False, True):
            when = w["d_late"] if late else w["d_early"] & (w["top"] != near)

            @pl.when(w[parity] & when)
            def _():
                for j in range(4):
                    emit(j, at(j, near, late))


def middle_kernel(late, held, base, a_low, inv, *refs):
    w = role()
    if late:
        ra, rb, rc, rd, _, _, _, sb, diag1, low1, s_far = refs
    else:
        (ra, rb, sb, diag1, low1, s_far), rc, rd = refs, None, None

    def emit(j, total):
        old = held[DIAG + j]
        one = old + (total - old)
        diag1[j] = one
        value = one.astype(BF16)
        sb[j] = value
        if not late:
            s_far[j] = value

    each_diagonal(w, late, emit, base, held, rb, ra, rc, rd)

    def lower(dst, u, j, s):
        one = lower_step(held[s], a_low[s - X], u[j], inv[w["off"] + j])
        low1[s - X] = one
        dst[s - OFF if s > X else 4] = one.astype(BF16)

    if late:

        @pl.when(w["f_late"])
        def _():
            for j in range(4):
                lower(s_far, rc, j, OFF + j)

    else:

        @pl.when(w["n_even"])
        def _():
            for j in range(4):
                lower(sb, ra, j, OFF + j)
            lower(sb, ra, 3, X)


def between_kernel(held, diag1, left1, a_low, inv, keep, rb, done_up, done_right, out, low1, zeros, done, sems):
    w = role()
    zeros[...] = jnp.zeros_like(zeros)
    rows = zeros.shape[0]
    fill = Copies(sems.at[0])
    for k in range(out.shape[0] // rows):
        fill.add(None, zeros, out.at[pl.ds(k * rows, rows)])
    fill.run(True)
    writes = Copies(sems.at[1])
    for s in range(OFF, HELD):
        writes.add(w["upper"], done_up.at[s - X], block(out, *spot(w, s)))
    writes.add(w["near_upper"], done_up.at[0], block(out, *spot(w, X)))
    for j, place in enumerate(right_of(w)):
        writes.add(w["d"], done_right.at[j], block(out, *place))
    for j in range(3):
        writes.add(w["d"], done.at[j], block(out, j + 1, w["first"] + j))

    @pl.when(w["d"])
    def _():
        for j in range(3):
            u = diag1[j].astype(BF16)
            two = lower_step(left1[j], a_low[5 + j], u, inv[w["first"] + j])
            done[j] = two * keep[5 + j, 0:1, :]

    @pl.when(w["d_odd"])
    def _():
        for j in range(4):
            low1[1 + j] = lower_step(held[OFF + j], a_low[1 + j], rb[j], inv[w["off"] + j])
        low1[0] = lower_step(held[X], a_low[0], rb[3], inv[w["off"] + 3])

    fill.run(False)
    writes.run(True)
    writes.run(False)


def last_kernel(late, diag1, base2, low1, low1_d, a_low, inv, keep, *refs):
    w = role()
    if late:
        ra, rb, r5, r7, rd, _, out, done, sem = refs
    else:
        (ra, rb, _, out, done, sem), r7, rd = refs, None, None
    writes = Copies(sem)
    for j in range(4):
        writes.add(w["d_late" if late else "d_early"], done.at[j], block(out, *spot(w, j)))
    for s in range(OFF, HELD):
        writes.add(w["f_late" if late else "near_lower"], done.at[s], block(out, *spot(w, s)))
    if not late:
        writes.add(w["near_lower"], done.at[X], block(out, *spot(w, X)))

    class Own:
        def __getitem__(self, s):
            return low1_d[s - X]

    def emit(j, total):
        old = diag1[j]
        done[DIAG + j] = old + (total - old)

    each_diagonal(w, late, emit, base2, Own(), rb, ra, r7, rd)

    def lower(old, u, j, s):
        two = lower_step(old[s - X], a_low[s - X], u[j], inv[w["off"] + j])
        done[s] = two * keep[s - X, 0:1, :]

    for name, old, u in (("f_late", low1, r5),) if late else (("d_odd", low1_d, rb), ("n_even", low1, rb)):

        @pl.when(w[name])
        def _():
            for j in range(4):
                lower(old, u, j, OFF + j)
            if not late:
                lower(old, u, 3, X)

    writes.run(True)
    writes.run(False)


def needed():
    def at(r, c):
        return r * 8 + c

    diag = [at(r, r // 2) for r in range(16)]
    near = {r: at(r, r // 2 + (1 if r % 2 else -1)) for r in range(1, 15)}
    far = [at(r, r // 2 + (4 if r < 8 else -4)) for r in range(16)]
    pair = [(diag[r], diag[r + 1]) for r in range(0, 16, 2)]
    up = [(near[r], diag[r + 1]) for r in range(1, 14, 2)]
    low = [(near[r], diag[r]) for r in range(2, 15, 2)]
    onward = [(diag[r], near[r + 1]) for r in range(1, 14, 2)]
    down = [(diag[r], far[r + 8]) for r in range(8)]
    far_l = [(far[r], diag[r]) for r in range(8, 16)]
    far_u = [(far[r], diag[r + 8]) for r in range(8)]
    return {
        "l": pair + low,
        "u": pair + up + onward,
        "far_l": down + far_l,
        "far_u": far_u,
        "u2": pair + up,
        "far_u2": far_u,
        "l2": pair + low + onward,
        "down": down,
        "far_l2": far_l,
    }


RECEIVERS = {
    "l": [
        8, 41, 10, 11, 12, 13, 31, 15, 9, 1, 2, 3, 4, 5, 6, 7,
        17, 25, 26, 27, 28, 29, 24, 30, 16, 0, 18, 19, 20, 21, 22, 23,
        40, 34, 42, 58, 37, 43, 46, 79, 32, 33, 44, 35, 45, 47, 38, 39,
        88, 56, 51, 59, 60, 61, 62, 63, 48, 49, 50, 57, 52, 53, 54, 55,
        72, 73, 74, 68, 76, 77, 78, 111, 64, 65, 66, 67, 36, 69, 70, 71,
        94, 89, 75, 90, 85, 93, 92, 95, 80, 81, 82, 83, 84, 91, 86, 87,
        104, 105, 106, 107, 108, 102, 110, 126, 96, 97, 98, 99, 100, 101, 14, 103,
        120, 121, 122, 123, 109, 124, 119, 127, 112, 113, 114, 115, 116, 117, 118, 125,
    ],
    "u": [
        8, 9, 10, 11, 12, 13, 0, 15, 16, 17, 2, 3, 4, 5, 6, 7,
        24, 25, 26, 27, 28, 29, 30, 31, 18, 33, 34, 19, 20, 21, 22, 14,
        40, 41, 42, 43, 44, 45, 46, 47, 32, 1, 50, 51, 36, 37, 38, 39,
        56, 57, 58, 59, 60, 61, 62, 63, 48, 49, 52, 67, 68, 53, 54, 55,
        72, 73, 74, 75, 76, 77, 78, 79, 64, 65, 66, 35, 84, 85, 70, 71,
        88, 89, 90, 91, 92, 93, 94, 95, 80, 81, 82, 83, 86, 101, 102, 87,
        104, 105, 106, 107, 108, 109, 110, 111, 96, 97, 98, 99, 100, 69, 118, 119,
        120, 121, 122, 123, 124, 125, 126, 127, 112, 113, 114, 115, 116, 117, 103, 23,
    ],
    "far_l": [
        64, 9, 10, 11, 12, 13, 14, 15, 72, 1, 2, 3, 4, 5, 6, 7,
        24, 81, 26, 27, 28, 29, 30, 25, 16, 89, 18, 19, 20, 21, 22, 17,
        40, 41, 98, 43, 42, 45, 46, 47, 32, 33, 106, 35, 34, 37, 38, 39,
        56, 57, 58, 115, 60, 59, 62, 63, 48, 49, 50, 123, 52, 51, 54, 55,
        68, 73, 74, 75, 36, 77, 78, 79, 76, 65, 66, 67, 44, 69, 70, 71,
        88, 85, 90, 91, 92, 53, 94, 95, 80, 93, 82, 83, 84, 61, 86, 87,
        8, 105, 102, 107, 108, 109, 104, 111, 0, 97, 110, 99, 100, 101, 96, 103,
        120, 121, 122, 119, 124, 125, 126, 23, 112, 113, 114, 127, 116, 117, 118, 31,
    ],
    "far_u": [
        8, 9, 10, 11, 68, 13, 14, 15, 0, 1, 2, 3, 76, 5, 6, 7,
        24, 25, 26, 27, 28, 85, 30, 63, 16, 17, 18, 19, 20, 93, 22, 23,
        40, 41, 42, 43, 44, 45, 102, 47, 32, 33, 34, 35, 38, 37, 110, 39,
        56, 57, 58, 59, 60, 61, 62, 119, 48, 49, 50, 51, 52, 55, 54, 127,
        72, 73, 74, 75, 36, 77, 78, 79, 64, 65, 66, 67, 100, 69, 46, 71,
        88, 89, 90, 91, 92, 117, 94, 95, 80, 81, 82, 83, 84, 53, 86, 87,
        104, 105, 106, 107, 4, 109, 70, 111, 96, 97, 98, 99, 12, 101, 108, 103,
        120, 121, 122, 123, 124, 21, 126, 31, 112, 113, 114, 115, 116, 29, 118, 125,
    ],
    "u2": [
        8, 9, 10, 11, 12, 13, 14, 15, 0, 17, 2, 3, 4, 5, 1, 7,
        24, 25, 26, 27, 28, 29, 30, 31, 16, 19, 34, 18, 20, 21, 22, 6,
        40, 41, 42, 43, 44, 45, 46, 47, 32, 33, 35, 51, 36, 37, 38, 39,
        56, 57, 58, 59, 60, 61, 62, 63, 48, 49, 50, 53, 68, 52, 54, 55,
        72, 73, 74, 75, 76, 77, 78, 79, 64, 65, 66, 67, 69, 85, 70, 71,
        88, 89, 90, 91, 92, 93, 94, 95, 80, 81, 82, 83, 84, 87, 102, 86,
        104, 105, 106, 107, 108, 109, 110, 111, 96, 97, 98, 99, 100, 101, 103, 119,
        120, 121, 122, 123, 124, 125, 126, 127, 112, 113, 114, 115, 116, 117, 118, 23,
    ],
    "far_u2": [
        8, 9, 10, 11, 68, 13, 38, 15, 0, 1, 2, 3, 76, 5, 46, 7,
        24, 25, 26, 27, 28, 85, 30, 63, 16, 17, 18, 19, 20, 93, 22, 55,
        40, 41, 42, 43, 44, 45, 102, 47, 32, 33, 34, 35, 36, 37, 110, 39,
        56, 57, 58, 59, 60, 61, 62, 119, 48, 49, 50, 51, 52, 53, 54, 127,
        72, 73, 74, 75, 100, 77, 78, 79, 64, 65, 66, 67, 108, 69, 70, 71,
        88, 89, 90, 91, 92, 125, 94, 95, 80, 81, 82, 83, 84, 117, 86, 87,
        104, 105, 106, 107, 12, 109, 14, 111, 96, 97, 98, 99, 4, 101, 6, 103,
        120, 121, 122, 123, 124, 21, 126, 23, 112, 113, 114, 115, 116, 29, 118, 31,
    ],
    "l2": [
        8, 9, 10, 11, 12, 13, 14, 15, 16, 1, 2, 3, 4, 5, 6, 7,
        17, 25, 26, 27, 28, 29, 30, 31, 58, 33, 18, 19, 20, 21, 22, 23,
        40, 34, 42, 43, 44, 45, 46, 47, 0, 32, 50, 35, 36, 37, 38, 39,
        56, 57, 51, 59, 60, 61, 62, 63, 48, 49, 92, 67, 52, 53, 54, 55,
        72, 73, 74, 68, 76, 77, 78, 79, 64, 65, 66, 41, 84, 69, 70, 71,
        88, 89, 90, 91, 85, 93, 94, 95, 80, 81, 82, 83, 109, 101, 86, 87,
        104, 105, 106, 107, 108, 102, 110, 111, 96, 97, 98, 99, 100, 75, 118, 103,
        120, 121, 122, 123, 124, 125, 119, 127, 112, 113, 114, 115, 116, 117, 24, 126,
    ],
    "down": [
        64, 9, 42, 11, 12, 13, 14, 15, 72, 1, 34, 3, 4, 5, 6, 7,
        24, 81, 26, 59, 28, 29, 30, 31, 16, 89, 18, 51, 20, 21, 22, 23,
        40, 41, 98, 43, 44, 45, 46, 47, 32, 33, 106, 35, 36, 37, 38, 39,
        56, 57, 58, 115, 60, 61, 62, 63, 48, 49, 50, 123, 52, 53, 54, 55,
        104, 73, 74, 75, 76, 77, 78, 79, 96, 65, 66, 67, 68, 69, 70, 71,
        88, 113, 90, 91, 92, 93, 94, 95, 80, 121, 82, 83, 84, 85, 86, 87,
        0, 105, 10, 107, 108, 109, 110, 111, 8, 97, 2, 99, 100, 101, 102, 103,
        120, 17, 122, 27, 124, 125, 126, 127, 112, 25, 114, 19, 116, 117, 118, 119,
    ],
    "far_l2": [
        8, 9, 10, 11, 12, 13, 14, 15, 0, 1, 2, 3, 4, 5, 6, 7,
        24, 25, 26, 27, 28, 29, 30, 31, 16, 17, 18, 19, 20, 21, 22, 23,
        40, 41, 42, 43, 44, 45, 46, 47, 32, 33, 34, 35, 36, 37, 38, 39,
        56, 57, 58, 59, 60, 61, 62, 63, 48, 49, 50, 51, 52, 53, 54, 55,
        68, 73, 74, 75, 66, 77, 78, 79, 76, 65, 64, 67, 108, 69, 70, 71,
        88, 85, 90, 91, 92, 83, 94, 95, 80, 93, 82, 123, 84, 117, 86, 81,
        98, 105, 102, 107, 106, 109, 104, 111, 72, 97, 110, 99, 100, 101, 96, 103,
        120, 121, 122, 119, 124, 125, 126, 113, 112, 89, 114, 127, 116, 115, 118, 87,
    ],
}


def move(name, buffer):
    return lax.ppermute(buffer, ("row", "col"), ROUTES[name])


ROUTES = {name: list(enumerate(to)) for name, to in RECEIVERS.items()}
for name, pairs in needed().items():
    assert set(pairs) <= set(ROUTES[name]), name
ANY = pl.BlockSpec(memory_space=pl.ANY)
VM = pl.BlockSpec(memory_space=pltpu.VMEM)
MIB = 1 << 20


def wide(n):
    return jax.ShapeDtypeStruct((n, BS, BS), F32)


def half(n):
    return jax.ShapeDtypeStruct((n, BS, BS), BF16)


SENT = [half(5), half(5), half(4), half(4)]
FAR_ROWS, DOWN_ROWS = 6, 6


def call(kernel, name, out_shape, in_specs, out_specs, scratch, aliases=None, cost=None):
    return pl.pallas_call(
        kernel,
        out_shape=out_shape,
        in_specs=in_specs,
        out_specs=out_specs,
        scratch_shapes=scratch,
        input_output_aliases=aliases or {},
        compiler_params=pltpu.CompilerParams(vmem_limit_bytes=20 * MIB),
        cost_estimate=cost and pl.CostEstimate(flops=cost[0], bytes_accessed=cost[1], transcendentals=0),
        name=name,
    )


def on_device(matrix, factors, inverse, pattern, dropped):
    matrix, factors, inverse, pattern, dropped = (
        pltpu.with_memory_space_constraint(x, pltpu.HBM)
        for x in (matrix, factors, inverse, pattern, dropped)
    )
    table = pltpu.SMEM(pattern.shape, jnp.int32)
    sem = pltpu.SemaphoreType.DMA
    whole_out = jax.ShapeDtypeStruct(factors.shape, F32)

    *sent, held = call(
        cut_kernel, "cut", [*SENT, wide(HELD)], [ANY] * 2, [VM] * 5, [table, sem, sem],
    )(pattern, factors)
    rb = move("l", sent[1])
    ra = move("u", sent[0])
    rc = move("far_l", sent[2])
    rd = move("far_u", sent[3])
    upper_b, upper_f, done_up = call(
        upper_kernel,
        "upper",
        [half(6), half(FAR_ROWS), wide(5)],
        [ANY] * 3 + [VM],
        [VM] * 3,
        [pltpu.VMEM((5, BS, BS), BF16), table, table, sem((2,))],
        cost=(10_000_000, 2_000_000),
    )(pattern, dropped, matrix, held)
    ra2 = move("u2", upper_b)
    rd2 = move("far_u2", upper_f)
    base, base2, a_low, left1, inv, keep, done_right = call(
        stage_kernel,
        "stage",
        [wide(4), wide(4), half(8), wide(3), half(inverse.shape[0]),
         jax.ShapeDtypeStruct((8, 8, BS), F32), wide(3)],
        [ANY] * 5 + [VM],
        [VM] * 7,
        [pltpu.VMEM((6, BS, BS), F32), pltpu.VMEM((15, BS, BS), BF16), table, table, sem((4,))],
        cost=(60_000_000, 6_000_000),
    )(pattern, dropped, factors, matrix, inverse, held)
    parts = [half(5), wide(4), wide(5)]
    *part, sent_down = call(
        functools.partial(middle_kernel, False), "early", [*parts, half(DOWN_ROWS)], [VM] * 6, [VM] * 4, [],
    )(held, base, a_low, inv, ra, rb)
    r5 = move("down", sent_down)
    sent_b, diag1, low1, sent_far = call(
        functools.partial(middle_kernel, True), "late", [*parts, half(4)], [VM] * 11, [VM] * 4, [],
        aliases={8: 0, 9: 1, 10: 2},
    )(held, base, a_low, inv, ra, rb, rc, rd, *part)
    rb2 = move("l2", sent_b)
    r7 = move("far_l2", sent_far)
    out, low1_d = call(
        between_kernel,
        "between",
        [whole_out, wide(5)],
        [VM] * 9,
        [ANY, VM],
        [pltpu.VMEM((64, factors.shape[1]), F32), pltpu.VMEM((3, BS, BS), F32), sem((2,))],
        cost=(60_000_000, 4_000_000),
    )(held, diag1, left1, a_low, inv, keep, rb, done_up, done_right)
    state = (diag1, base2, low1, low1_d, a_low, inv, keep, ra2, rb2)
    ends = [pltpu.VMEM((HELD, BS, BS), F32), sem]
    out = call(
        functools.partial(last_kernel, False), "last_early", whole_out, [VM] * 9 + [ANY], ANY, ends, aliases={9: 0},
    )(*state, out)
    return call(
        functools.partial(last_kernel, True), "last_late", whole_out, [VM] * 12 + [ANY], ANY, ends, aliases={12: 0},
    )(*state, r5, r7, rd2, out)


def solution(mesh):
    placed = (
        P("row", "col"),
        P("row", "col"),
        P("col", None, None),
        P("row", "col"),
        P("row", "col"),
    )
    return jax.shard_map(
        on_device, mesh=mesh, in_specs=placed, out_specs=P("row", "col"), check_vma=False
    )
```

```python
import functools

import jax
import jax.numpy as jnp
from jax import lax
from jax.experimental import pallas as pl
from jax.experimental.pallas import tpu as pltpu
from jax.sharding import PartitionSpec as P

BS = 128
F32 = jnp.float32
BF16 = jnp.bfloat16

DIAG, X, OFF = 0, 4, 5
HELD = 9


def role():
    r, c = lax.axis_index("row"), lax.axis_index("col")
    odd = lax.rem(r, 2)
    home = lax.div(r, 2)
    late = r >= 8
    is_odd = odd == 1
    even = odd == 0
    is_d = c == home
    is_n = jnp.where(is_odd, c == home + 1, c == home - 1)
    is_f = jnp.where(late, c == home - 4, c == home + 4)
    lower = (is_d & is_odd) | (is_n & even) | (is_f & late)
    held = is_d | is_n | is_f
    return dict(
        even=even,
        top=r == 0,
        d=is_d,
        d_even=is_d & even,
        d_odd=is_d & is_odd,
        d_late=is_d & late,
        d_early=is_d & jnp.logical_not(late),
        n_even=is_n & even,
        n_odd=is_n & is_odd,
        f=is_f,
        f_late=is_f & late,
        f_early=is_f & jnp.logical_not(late),
        near=is_d | is_n,
        any=held,
        lower=lower,
        near_lower=lower & jnp.logical_not(is_f),
        upper=held & jnp.logical_not(lower),
        near_upper=held & jnp.logical_not(lower) & jnp.logical_not(is_f),
        first=4 * odd,
        off=jnp.where(is_f, 4 * odd, 4 * (1 - odd)),
        x_row=jnp.where(is_odd, jnp.where(is_d, 0, 3), jnp.where(is_d, 3, 0)),
        x_col=jnp.where(is_odd, jnp.where(is_d, 3, 0), jnp.where(is_d, 4, 7)),
    )


def spot(w, slot):
    if slot == X:
        return w["x_row"], w["x_col"]
    if slot < X:
        return slot, w["first"] + slot
    return slot - OFF, w["off"] + slot - OFF


def block(ref, i, c):
    return ref.at[pl.ds(pl.multiple_of(i * BS, BS), BS), pl.ds(pl.multiple_of(c * BS, BS), BS)]


def dot(a, b):
    return jnp.dot(a, b, preferred_element_type=F32)


class Copies:
    def __init__(self, sem):
        self.sem, self.todo = sem, []

    def add(self, when, src, dst):
        self.todo.append((when, src, dst))

    def run(self, start):
        i = 0
        while i < len(self.todo):
            when = self.todo[i][0]
            j = i
            while j < len(self.todo) and self.todo[j][0] is when:
                j += 1
            some = self.todo[i:j]

            def act(some=some):
                for _, src, dst in some:
                    copy = pltpu.make_async_copy(src, dst, self.sem)
                    copy.start() if start else copy.wait()

            if when is None:
                act()
            else:
                pl.when(when)(act)
            i = j


def member(table, place):
    return (table[place] == 1).astype(F32)


def cut_kernel(pattern, factors, sa, sb, sc, sd, held, table, sem, table_sem):
    w = role()

    @pl.when(w["any"])
    def _():
        get_table = pltpu.make_async_copy(pattern, table, table_sem)
        get_table.start()
        blocks = Copies(sem)
        for s in range(HELD):
            when = w["d"] if s < X else w["near"] if s == X else None
            blocks.add(when, block(factors, *spot(w, s)), held.at[s])
        blocks.run(True)
        get_table.wait()
        blocks.run(False)

        def masked(s):
            value = held[s] * member(table, spot(w, s))
            held[s] = value
            return value.astype(BF16)

        @pl.when(w["d"])
        def _():
            for j in range(4):
                value = masked(DIAG + j)
                sc[j] = value

                @pl.when(w["even"])
                def _():
                    sb[j] = value

                @pl.when(w["d_odd"])
                def _():
                    sa[j] = value

        @pl.when(w["f_early"])
        def _():
            for j in range(4):
                sd[j] = masked(OFF + j)

        @pl.when(w["f_late"])
        def _():
            for j in range(4):
                sc[j] = masked(OFF + j)

        @pl.when(w["d_even"] | w["n_odd"])
        def _():
            for j in range(4):
                sa[j] = masked(OFF + j)
            sa[4] = masked(X)

        @pl.when(w["n_even"])
        def _():
            for j in range(4):
                sb[j] = masked(OFF + j)
            sb[4] = masked(X)

        @pl.when(w["d_odd"])
        def _():
            for j in range(4):
                masked(OFF + j)
            masked(X)


def kept(drops, place):
    return (1 - drops[place]).astype(F32)


def upper(table, drops, old, a_block, place):
    m = member(table, place)
    a_block = a_block.astype(F32)
    one = old + (a_block - old) * m
    return one, (one + (a_block - one) * m) * kept(drops, place)


def upper_kernel(pattern, dropped, matrix, held, upper_b, upper_f, done, a, table, drops, sems):
    w = role()

    @pl.when(w["upper"])
    def _():
        loads = Copies(sems.at[0])
        loads.add(None, pattern, table)
        loads.add(None, dropped, drops)
        blocks = Copies(sems.at[1])
        for s in range(OFF, HELD):
            blocks.add(None, block(matrix, *spot(w, s)), a.at[s - X])
        blocks.add(w["near_upper"], block(matrix, *spot(w, X)), a.at[0])
        loads.run(True)
        blocks.run(True)
        loads.run(False)
        blocks.run(False)
        for s in range(X, HELD):

            def act(s=s):
                one, done[s - X] = upper(table, drops, held[s], a[s - X], spot(w, s))
                one = one.astype(BF16)
                upper_b[s - OFF if s > X else 4] = one
                if s > X:
                    upper_f[s - OFF] = one

            act() if s > X else pl.when(w["near_upper"])(act)


def right_of(w):
    return [(j, w["first"] + j + 1) for j in range(3)]


def stage_kernel(pattern, dropped, factors, matrix, inverse, held,
                 base, base2, a_low, left1, inv, keep, done,
                 f, a, table, drops, sems):
    w = role()
    tables = Copies(sems.at[1])
    tables.add(None, pattern, table)
    tables.add(None, dropped, drops)
    blocks = Copies(sems.at[2])
    right = right_of(w)
    left = [(j + 1, w["first"] + j) for j in range(3)]
    for k, place in enumerate(right + left):
        blocks.add(w["d"], block(factors, *place), f.at[k])
    for s in range(X):
        blocks.add(w["d"], block(matrix, *spot(w, s)), a.at[s])
    for k, place in enumerate(right + left):
        blocks.add(w["d"], block(matrix, *place), a.at[HELD + k])
    blocks.add(w["near_lower"], block(matrix, *spot(w, X)), a.at[X])
    for s in range(OFF, HELD):
        blocks.add(w["lower"], block(matrix, *spot(w, s)), a.at[s])
    blocks.add(None, inverse, inv)

    @pl.when(w["any"])
    def _():
        tables.run(True)
        blocks.run(True)
        tables.run(False)
        blocks.run(False)

        @pl.when(w["lower"])
        def _():
            for s in range(X, HELD):

                def act(s=s):
                    place = spot(w, s)
                    a_low[s - X] = (a[s].astype(F32) * member(table, place)).astype(BF16)
                    keep[s - X] = jnp.full(keep.shape[1:], kept(drops, place))

                act() if s > X else pl.when(w["near_lower"])(act)

        @pl.when(w["d"])
        def _():
            base[0] = a[0].astype(F32)
            base2[0] = a[0].astype(F32)
            for j in range(3):
                old_u = f[j] * member(table, right[j])
                one_u, done[j] = upper(table, drops, old_u, a[HELD + j], right[j])
                m = member(table, left[j])
                old = f[3 + j] * m
                old_b = old.astype(BF16)
                a_block = a[HELD + 3 + j].astype(F32) * m
                residual = a_block - dot(old_b, held[DIAG + j].astype(BF16)) * m
                one = old + dot(residual.astype(BF16), inv[w["first"] + j]) * m
                left1[j] = one
                a_low[5 + j] = a_block.astype(BF16)
                keep[5 + j] = jnp.full(keep.shape[1:], kept(drops, left[j]))
                a_diag = a[j + 1].astype(F32)
                base[j + 1] = a_diag - dot(old_b, old_u.astype(BF16))
                base2[j + 1] = a_diag - dot(one.astype(BF16), one_u.astype(BF16))


def diagonal(w, sums, l_near, l_x, ra, rc, rd):
    def at(j, with_near, with_far):
        total = sums[j]
        if with_near:
            total = total - dot(l_near(j), ra[j])
        if with_near and j == 0:
            total = total - dot(l_x(), ra[4])
        if with_far:
            total = total - dot(rc[j], rd[j])
        return total

    return at


def lower_step(old, a_block, u, inv_block):
    residual = a_block.astype(F32) - dot(old.astype(BF16), u)
    return old + dot(residual.astype(BF16), inv_block)


def each_diagonal(w, late, emit, sums, own, rb, ra, rc, rd):
    for parity, l_near, l_x in (
        ("d_even", lambda j: rb[j], lambda: rb[4]),
        ("d_odd", lambda j: own[OFF + j].astype(BF16), lambda: own[X].astype(BF16)),
    ):
        at = diagonal(w, sums, l_near, l_x, ra, rc, rd)
        for near in (True,) if late or parity == "d_odd" else (False, True):
            when = w["d_late"] if late else w["d_early"] & (w["top"] != near)

            @pl.when(w[parity] & when)
            def _():
                for j in range(4):
                    emit(j, at(j, near, late))


def middle_kernel(late, held, base, a_low, inv, *refs):
    w = role()
    if late:
        ra, rb, rc, rd, _, _, _, sb, diag1, low1, s_far = refs
    else:
        (ra, rb, sb, diag1, low1, s_far), rc, rd = refs, None, None

    def emit(j, total):
        old = held[DIAG + j]
        one = old + (total - old)
        diag1[j] = one
        value = one.astype(BF16)
        sb[j] = value
        if not late:
            s_far[j] = value

    each_diagonal(w, late, emit, base, held, rb, ra, rc, rd)

    def lower(dst, u, j, s):
        one = lower_step(held[s], a_low[s - X], u[j], inv[w["off"] + j])
        low1[s - X] = one
        dst[s - OFF if s > X else 4] = one.astype(BF16)

    if late:

        @pl.when(w["f_late"])
        def _():
            for j in range(4):
                lower(s_far, rc, j, OFF + j)

    else:

        @pl.when(w["n_even"])
        def _():
            for j in range(4):
                lower(sb, ra, j, OFF + j)
            lower(sb, ra, 3, X)


def between_kernel(held, diag1, left1, a_low, inv, keep, rb, done_up, done_right, out, low1, zeros, done, sems):
    w = role()
    zeros[...] = jnp.zeros_like(zeros)
    rows = zeros.shape[0]
    fill = Copies(sems.at[0])
    for k in range(out.shape[0] // rows):
        fill.add(None, zeros, out.at[pl.ds(k * rows, rows)])
    fill.run(True)
    writes = Copies(sems.at[1])
    for s in range(OFF, HELD):
        writes.add(w["upper"], done_up.at[s - X], block(out, *spot(w, s)))
    writes.add(w["near_upper"], done_up.at[0], block(out, *spot(w, X)))
    for j, place in enumerate(right_of(w)):
        writes.add(w["d"], done_right.at[j], block(out, *place))
    for j in range(3):
        writes.add(w["d"], done.at[j], block(out, j + 1, w["first"] + j))

    @pl.when(w["d"])
    def _():
        for j in range(3):
            u = diag1[j].astype(BF16)
            two = lower_step(left1[j], a_low[5 + j], u, inv[w["first"] + j])
            done[j] = two * keep[5 + j, 0:1, :]

    @pl.when(w["d_odd"])
    def _():
        for j in range(4):
            low1[1 + j] = lower_step(held[OFF + j], a_low[1 + j], rb[j], inv[w["off"] + j])
        low1[0] = lower_step(held[X], a_low[0], rb[3], inv[w["off"] + 3])

    fill.run(False)
    writes.run(True)
    writes.run(False)


def last_kernel(late, diag1, base2, low1, low1_d, a_low, inv, keep, *refs):
    w = role()
    if late:
        ra, rb, r5, r7, rd, _, out, done, sem = refs
    else:
        (ra, rb, _, out, done, sem), r7, rd = refs, None, None
    writes = Copies(sem)
    for j in range(4):
        writes.add(w["d_late" if late else "d_early"], done.at[j], block(out, *spot(w, j)))
    for s in range(OFF, HELD):
        writes.add(w["f_late" if late else "near_lower"], done.at[s], block(out, *spot(w, s)))
    if not late:
        writes.add(w["near_lower"], done.at[X], block(out, *spot(w, X)))

    class Own:
        def __getitem__(self, s):
            return low1_d[s - X]

    def emit(j, total):
        old = diag1[j]
        done[DIAG + j] = old + (total - old)
        pltpu.make_async_copy(done.at[j], block(out, *spot(w, j)), sem).start()

    each_diagonal(w, late, emit, base2, Own(), rb, ra, r7, rd)

    def lower(old, u, j, s):
        two = lower_step(old[s - X], a_low[s - X], u[j], inv[w["off"] + j])
        done[s] = two * keep[s - X, 0:1, :]
        pltpu.make_async_copy(done.at[s], block(out, *spot(w, s)), sem).start()

    for name, old, u in (("f_late", low1, r5),) if late else (("d_odd", low1_d, rb), ("n_even", low1, rb)):

        @pl.when(w[name])
        def _():
            for j in range(4):
                lower(old, u, j, OFF + j)
            if not late:
                lower(old, u, 3, X)

    writes.run(False)


def needed():
    def at(r, c):
        return r * 8 + c

    diag = [at(r, r // 2) for r in range(16)]
    near = {r: at(r, r // 2 + (1 if r % 2 else -1)) for r in range(1, 15)}
    far = [at(r, r // 2 + (4 if r < 8 else -4)) for r in range(16)]
    pair = [(diag[r], diag[r + 1]) for r in range(0, 16, 2)]
    up = [(near[r], diag[r + 1]) for r in range(1, 14, 2)]
    low = [(near[r], diag[r]) for r in range(2, 15, 2)]
    onward = [(diag[r], near[r + 1]) for r in range(1, 14, 2)]
    down = [(diag[r], far[r + 8]) for r in range(8)]
    far_l = [(far[r], diag[r]) for r in range(8, 16)]
    far_u = [(far[r], diag[r + 8]) for r in range(8)]
    return {
        "l": pair + low,
        "u": pair + up + onward,
        "far_l": down + far_l,
        "far_u": far_u,
        "u2": pair + up,
        "far_u2": far_u,
        "l2": pair + low + onward,
        "down": down,
        "far_l2": far_l,
    }


RECEIVERS = {
    "l": [
        8, 41, 10, 11, 12, 13, 31, 15, 9, 1, 2, 3, 4, 5, 6, 7,
        17, 25, 26, 27, 28, 29, 24, 30, 16, 0, 18, 19, 20, 21, 22, 23,
        40, 34, 42, 58, 37, 43, 46, 79, 32, 33, 44, 35, 45, 47, 38, 39,
        88, 56, 51, 59, 60, 61, 62, 63, 48, 49, 50, 57, 52, 53, 54, 55,
        72, 73, 74, 68, 76, 77, 78, 111, 64, 65, 66, 67, 36, 69, 70, 71,
        94, 89, 75, 90, 85, 93, 92, 95, 80, 81, 82, 83, 84, 91, 86, 87,
        104, 105, 106, 107, 108, 102, 110, 126, 96, 97, 98, 99, 100, 101, 14, 103,
        120, 121, 122, 123, 109, 124, 119, 127, 112, 113, 114, 115, 116, 117, 118, 125,
    ],
    "u": [
        8, 9, 10, 11, 12, 13, 0, 15, 16, 17, 2, 3, 4, 5, 6, 7,
        24, 25, 26, 27, 28, 29, 30, 31, 18, 33, 34, 19, 20, 21, 22, 14,
        40, 41, 42, 43, 44, 45, 46, 47, 32, 1, 50, 51, 36, 37, 38, 39,
        56, 57, 58, 59, 60, 61, 62, 63, 48, 49, 52, 67, 68, 53, 54, 55,
        72, 73, 74, 75, 76, 77, 78, 79, 64, 65, 66, 35, 84, 85, 70, 71,
        88, 89, 90, 91, 92, 93, 94, 95, 80, 81, 82, 83, 86, 101, 102, 87,
        104, 105, 106, 107, 108, 109, 110, 111, 96, 97, 98, 99, 100, 69, 118, 119,
        120, 121, 122, 123, 124, 125, 126, 127, 112, 113, 114, 115, 116, 117, 103, 23,
    ],
    "far_l": [
        64, 9, 10, 11, 12, 13, 14, 15, 72, 1, 2, 3, 4, 5, 6, 7,
        24, 81, 26, 27, 28, 29, 30, 25, 16, 89, 18, 19, 20, 21, 22, 17,
        40, 41, 98, 43, 42, 45, 46, 47, 32, 33, 106, 35, 34, 37, 38, 39,
        56, 57, 58, 115, 60, 59, 62, 63, 48, 49, 50, 123, 52, 51, 54, 55,
        68, 73, 74, 75, 36, 77, 78, 79, 76, 65, 66, 67, 44, 69, 70, 71,
        88, 85, 90, 91, 92, 53, 94, 95, 80, 93, 82, 83, 84, 61, 86, 87,
        8, 105, 102, 107, 108, 109, 104, 111, 0, 97, 110, 99, 100, 101, 96, 103,
        120, 121, 122, 119, 124, 125, 126, 23, 112, 113, 114, 127, 116, 117, 118, 31,
    ],
    "far_u": [
        8, 9, 10, 11, 68, 13, 14, 15, 0, 1, 2, 3, 76, 5, 6, 7,
        24, 25, 26, 27, 28, 85, 30, 63, 16, 17, 18, 19, 20, 93, 22, 23,
        40, 41, 42, 43, 44, 45, 102, 47, 32, 33, 34, 35, 38, 37, 110, 39,
        56, 57, 58, 59, 60, 61, 62, 119, 48, 49, 50, 51, 52, 55, 54, 127,
        72, 73, 74, 75, 36, 77, 78, 79, 64, 65, 66, 67, 100, 69, 46, 71,
        88, 89, 90, 91, 92, 117, 94, 95, 80, 81, 82, 83, 84, 53, 86, 87,
        104, 105, 106, 107, 4, 109, 70, 111, 96, 97, 98, 99, 12, 101, 108, 103,
        120, 121, 122, 123, 124, 21, 126, 31, 112, 113, 114, 115, 116, 29, 118, 125,
    ],
    "u2": [
        8, 9, 10, 11, 12, 13, 14, 15, 0, 17, 2, 3, 4, 5, 1, 7,
        24, 25, 26, 27, 28, 29, 30, 31, 16, 19, 34, 18, 20, 21, 22, 6,
        40, 41, 42, 43, 44, 45, 46, 47, 32, 33, 35, 51, 36, 37, 38, 39,
        56, 57, 58, 59, 60, 61, 62, 63, 48, 49, 50, 53, 68, 52, 54, 55,
        72, 73, 74, 75, 76, 77, 78, 79, 64, 65, 66, 67, 69, 85, 70, 71,
        88, 89, 90, 91, 92, 93, 94, 95, 80, 81, 82, 83, 84, 87, 102, 86,
        104, 105, 106, 107, 108, 109, 110, 111, 96, 97, 98, 99, 100, 101, 103, 119,
        120, 121, 122, 123, 124, 125, 126, 127, 112, 113, 114, 115, 116, 117, 118, 23,
    ],
    "far_u2": [
        8, 9, 10, 11, 68, 13, 38, 15, 0, 1, 2, 3, 76, 5, 46, 7,
        24, 25, 26, 27, 28, 85, 30, 63, 16, 17, 18, 19, 20, 93, 22, 55,
        40, 41, 42, 43, 44, 45, 102, 47, 32, 33, 34, 35, 36, 37, 110, 39,
        56, 57, 58, 59, 60, 61, 62, 119, 48, 49, 50, 51, 52, 53, 54, 127,
        72, 73, 74, 75, 100, 77, 78, 79, 64, 65, 66, 67, 108, 69, 70, 71,
        88, 89, 90, 91, 92, 125, 94, 95, 80, 81, 82, 83, 84, 117, 86, 87,
        104, 105, 106, 107, 12, 109, 14, 111, 96, 97, 98, 99, 4, 101, 6, 103,
        120, 121, 122, 123, 124, 21, 126, 23, 112, 113, 114, 115, 116, 29, 118, 31,
    ],
    "l2": [
        8, 9, 10, 11, 12, 13, 14, 15, 16, 1, 2, 3, 4, 5, 6, 7,
        17, 25, 26, 27, 28, 29, 30, 31, 58, 33, 18, 19, 20, 21, 22, 23,
        40, 34, 42, 43, 44, 45, 46, 47, 0, 32, 50, 35, 36, 37, 38, 39,
        56, 57, 51, 59, 60, 61, 62, 63, 48, 49, 92, 67, 52, 53, 54, 55,
        72, 73, 74, 68, 76, 77, 78, 79, 64, 65, 66, 41, 84, 69, 70, 71,
        88, 89, 90, 91, 85, 93, 94, 95, 80, 81, 82, 83, 109, 101, 86, 87,
        104, 105, 106, 107, 108, 102, 110, 111, 96, 97, 98, 99, 100, 75, 118, 103,
        120, 121, 122, 123, 124, 125, 119, 127, 112, 113, 114, 115, 116, 117, 24, 126,
    ],
    "down": [
        64, 9, 42, 11, 12, 13, 14, 15, 72, 1, 34, 3, 4, 5, 6, 7,
        24, 81, 26, 59, 28, 29, 30, 31, 16, 89, 18, 51, 20, 21, 22, 23,
        40, 41, 98, 43, 44, 45, 46, 47, 32, 33, 106, 35, 36, 37, 38, 39,
        56, 57, 58, 115, 60, 61, 62, 63, 48, 49, 50, 123, 52, 53, 54, 55,
        104, 73, 74, 75, 76, 77, 78, 79, 96, 65, 66, 67, 68, 69, 70, 71,
        88, 113, 90, 91, 92, 93, 94, 95, 80, 121, 82, 83, 84, 85, 86, 87,
        0, 105, 10, 107, 108, 109, 110, 111, 8, 97, 2, 99, 100, 101, 102, 103,
        120, 17, 122, 27, 124, 125, 126, 127, 112, 25, 114, 19, 116, 117, 118, 119,
    ],
    "far_l2": [
        8, 9, 10, 11, 12, 13, 14, 15, 0, 1, 2, 3, 4, 5, 6, 7,
        24, 25, 26, 27, 28, 29, 30, 31, 16, 17, 18, 19, 20, 21, 22, 23,
        40, 41, 42, 43, 44, 45, 46, 47, 32, 33, 34, 35, 36, 37, 38, 39,
        56, 57, 58, 59, 60, 61, 62, 63, 48, 49, 50, 51, 52, 53, 54, 55,
        68, 73, 74, 75, 66, 77, 78, 79, 76, 65, 64, 67, 108, 69, 70, 71,
        88, 85, 90, 91, 92, 83, 94, 95, 80, 93, 82, 123, 84, 117, 86, 81,
        98, 105, 102, 107, 106, 109, 104, 111, 72, 97, 110, 99, 100, 101, 96, 103,
        120, 121, 122, 119, 124, 125, 126, 113, 112, 89, 114, 127, 116, 115, 118, 87,
    ],
}


def move(name, buffer):
    return lax.ppermute(buffer, ("row", "col"), ROUTES[name])


ROUTES = {name: list(enumerate(to)) for name, to in RECEIVERS.items()}
for name, pairs in needed().items():
    assert set(pairs) <= set(ROUTES[name]), name
ANY = pl.BlockSpec(memory_space=pl.ANY)
VM = pl.BlockSpec(memory_space=pltpu.VMEM)
MIB = 1 << 20


def wide(n):
    return jax.ShapeDtypeStruct((n, BS, BS), F32)


def half(n):
    return jax.ShapeDtypeStruct((n, BS, BS), BF16)


SENT = [half(5), half(5), half(4), half(4)]
FAR_ROWS, DOWN_ROWS = 6, 6


def call(kernel, name, out_shape, in_specs, out_specs, scratch, aliases=None, cost=None):
    return pl.pallas_call(
        kernel,
        out_shape=out_shape,
        in_specs=in_specs,
        out_specs=out_specs,
        scratch_shapes=scratch,
        input_output_aliases=aliases or {},
        compiler_params=pltpu.CompilerParams(vmem_limit_bytes=20 * MIB),
        cost_estimate=cost and pl.CostEstimate(flops=cost[0], bytes_accessed=cost[1], transcendentals=0),
        name=name,
    )


def on_device(matrix, factors, inverse, pattern, dropped):
    matrix, factors, inverse, pattern, dropped = (
        pltpu.with_memory_space_constraint(x, pltpu.HBM)
        for x in (matrix, factors, inverse, pattern, dropped)
    )
    table = pltpu.SMEM(pattern.shape, jnp.int32)
    sem = pltpu.SemaphoreType.DMA
    whole_out = jax.ShapeDtypeStruct(factors.shape, F32)

    *sent, held = call(
        cut_kernel, "cut", [*SENT, wide(HELD)], [ANY] * 2, [VM] * 5, [table, sem, sem],
    )(pattern, factors)
    rb = move("l", sent[1])
    ra = move("u", sent[0])
    rc = move("far_l", sent[2])
    rd = move("far_u", sent[3])
    upper_b, upper_f, done_up = call(
        upper_kernel,
        "upper",
        [half(6), half(FAR_ROWS), wide(5)],
        [ANY] * 3 + [VM],
        [VM] * 3,
        [pltpu.VMEM((5, BS, BS), BF16), table, table, sem((2,))],
        cost=(10_000_000, 2_000_000),
    )(pattern, dropped, matrix, held)
    ra2 = move("u2", upper_b)
    rd2 = move("far_u2", upper_f)
    base, base2, a_low, left1, inv, keep, done_right = call(
        stage_kernel,
        "stage",
        [wide(4), wide(4), half(8), wide(3), half(inverse.shape[0]),
         jax.ShapeDtypeStruct((8, 8, BS), F32), wide(3)],
        [ANY] * 5 + [VM],
        [VM] * 7,
        [pltpu.VMEM((6, BS, BS), F32), pltpu.VMEM((15, BS, BS), BF16), table, table, sem((4,))],
        cost=(60_000_000, 6_000_000),
    )(pattern, dropped, factors, matrix, inverse, held)
    parts = [half(5), wide(4), wide(5)]
    *part, sent_down = call(
        functools.partial(middle_kernel, False), "early", [*parts, half(DOWN_ROWS)], [VM] * 6, [VM] * 4, [],
    )(held, base, a_low, inv, ra, rb)
    r5 = move("down", sent_down)
    sent_b, diag1, low1, sent_far = call(
        functools.partial(middle_kernel, True), "late", [*parts, half(4)], [VM] * 11, [VM] * 4, [],
        aliases={8: 0, 9: 1, 10: 2},
    )(held, base, a_low, inv, ra, rb, rc, rd, *part)
    rb2 = move("l2", sent_b)
    r7 = move("far_l2", sent_far)
    out, low1_d = call(
        between_kernel,
        "between",
        [whole_out, wide(5)],
        [VM] * 9,
        [ANY, VM],
        [pltpu.VMEM((64, factors.shape[1]), F32), pltpu.VMEM((3, BS, BS), F32), sem((2,))],
        cost=(60_000_000, 4_000_000),
    )(held, diag1, left1, a_low, inv, keep, rb, done_up, done_right)
    state = (diag1, base2, low1, low1_d, a_low, inv, keep, ra2, rb2)
    ends = [pltpu.VMEM((HELD, BS, BS), F32), sem]
    out = call(
        functools.partial(last_kernel, False), "last_early", whole_out, [VM] * 9 + [ANY], ANY, ends, aliases={9: 0},
    )(*state, out)
    return call(
        functools.partial(last_kernel, True), "last_late", whole_out, [VM] * 12 + [ANY], ANY, ends, aliases={12: 0},
    )(*state, r5, r7, rd2, out)


def solution(mesh):
    placed = (
        P("row", "col"),
        P("row", "col"),
        P("col", None, None),
        P("row", "col"),
        P("row", "col"),
    )
    return jax.shard_map(
        on_device, mesh=mesh, in_specs=placed, out_specs=P("row", "col"), check_vma=False
    )
```
